256 devices in a mesh: chan: 64 (over y, x, z_lo, core), feed: 4 (over z_hi).
Axes of the slice: x: 4, y: 4, z: 8 (z_hi: 4, z_lo: 2; z = z_hi * 2 + z_lo), core: 2. Of those that a mesh axis runs over, the one named last changes fastest.
Arguments:
- voltages: int32 [2048, 64, 2048], P('chan', 'feed'), may hold values from -128 to 127
- taper: float32 [4, 2048], replicated, may hold values from -3 to 3
- gains: int32 [2048, 128], P('chan'), may hold values from 16 to 79
Outputs:
- visibility: bfloat16 [128, 2, 2048, 2048], P('chan', None, 'feed')
The draws below stay inside these ranges and needn't reach their ends.
All inputs are finite; a program needn't handle non-finite values.
Results may differ from the reference program's by a relative error of at most 0.0057.
Values may be sent and summed in bfloat16 or wider, within the bound.
A program may use at most 64 MiB of HBM per device.

```python
import math
import jax
import jax.numpy as jnp
from jax import lax

NFFT = 2048
TAPS = 4
INPUTS = 2048
CHANNELS = 128
SPECTRA = 64


def set_ends(array, key, least, high):
    dims = array.shape
    place = [jax.random.randint(jax.random.fold_in(key, axis), (), 0, dims[axis]) for axis in range(len(dims))]
    array = array.at[tuple(place)].set(least)
    longest = dims.index(max(dims))
    place[longest] = (place[longest] + 1) % dims[longest]
    return array.at[tuple(place)].set(high)


def scatter_about(stream_key, shape, spread, bound, held_as=jnp.bfloat16):
    return jnp.clip(spread * jax.random.normal(stream_key, shape, jnp.float32), -bound, bound).astype(held_as)


def setup_inputs(seed: int = 0) -> dict:
    streams_of = jax.random.split(jax.random.key(seed), 4)
    voltages = set_ends(jax.random.randint(streams_of[0], (INPUTS, SPECTRA, NFFT), -128, 128), jax.random.fold_in(streams_of[0], 1), -128, 127).astype(jnp.int32)
    taper = scatter_about(streams_of[1], (TAPS, NFFT), 0.5, 3.0, jnp.float32)
    gains = set_ends(jax.random.randint(streams_of[2], (INPUTS, CHANNELS), 16, 80), jax.random.fold_in(streams_of[2], 1), 16, 79).astype(jnp.int32)
    return {"voltages": voltages, "taper": taper, "gains": gains}


def dft_table(points, count):
    positions = jnp.arange(points, dtype=jnp.int32)
    orders = jnp.arange(count, dtype=jnp.int32) + 1
    phase = positions[:, None] * orders[None, :] % points
    angle = phase.astype(jnp.float32) * (2.0 * math.pi / points)
    norm = 1.0 / math.sqrt(points)
    pair = jnp.stack([jnp.cos(angle) * norm, -jnp.sin(angle) * norm], axis=-1)
    return pair.reshape(points, 2 * count)

def reference(voltages, taper, gains):
    table = dft_table(NFFT, CHANNELS)
    blocks = INPUTS // 128
    grouped = voltages.reshape(blocks, 128, SPECTRA, NFFT)
    grouped_gains = gains.reshape(blocks, 128, CHANNELS)

    def filterbank(args):
        block, block_gains = args
        samples = block.astype(jnp.float32)
        front = jnp.zeros((128, TAPS - 1, NFFT), jnp.float32)
        extended = jnp.concatenate([front, samples], axis=1)
        total = jnp.zeros((128, SPECTRA, NFFT), jnp.float32)
        for tap in range(TAPS):
            total = total + taper[tap][None, None, :] * extended[:, tap:tap + SPECTRA, :]
        filtered = total * (1.0 / 64.0)
        spec = jnp.dot(filtered.reshape(128 * SPECTRA, NFFT), table, preferred_element_type=jnp.float32, precision=lax.Precision.HIGHEST)
        spec = spec.reshape(128, SPECTRA, CHANNELS, 2).transpose(2, 3, 1, 0)
        factor = (block_gains.astype(jnp.float32) / 64.0).T
        return (spec * factor[:, None, None, :]).astype(jnp.bfloat16)
    pieces = lax.map(filterbank, (grouped, grouped_gains))
    signals = pieces.transpose(1, 2, 3, 0, 4).reshape(CHANNELS, 2, SPECTRA, INPUTS)

    def correlate(channel):
        wide = channel.astype(jnp.float32)
        real_part = wide[0]
        imag_part = wide[1]
        left = jnp.stack([jnp.stack([real_part, imag_part]), jnp.stack([imag_part, -real_part])])
        summed = jnp.einsum('otsa,tsb->oab', left, wide)
        return (summed * (1.0 / SPECTRA)).astype(jnp.bfloat16)
    return lax.map(correlate, signals)
```

```python
import functools
import math

import jax
import jax.numpy as jnp
import numpy as np
from jax import lax
from jax.experimental import pallas as pl
from jax.experimental.pallas import tpu as pltpu
from jax.sharding import PartitionSpec as P

MESH = pl.DeviceIdType.MESH
F32, BF16 = jnp.float32, jnp.bfloat16

POINTS = 2048
HALF = POINTS // 2
CHANNELS = 128
IN_DEV = 32
SPECS = 16
TAPS = 4
COLUMNS = 16
RING = 8
SOURCES = 2 * COLUMNS
TILE = 16
LANES = 128
CHUNKS = 4
PIECE = SOURCES // CHUNKS


def tile_channel():
    parity, place = np.divmod(np.arange(2 * SOURCES), SOURCES)
    column, core = np.divmod(place, 2)
    return 2 * (column * 4 + parity * 2 + core)


def split_two(value):
    high = value.astype(jnp.bfloat16)
    low = (value - high.astype(np.float64)).astype(jnp.bfloat16)
    return high, low


def constants():
    first = tile_channel()
    position = np.arange(HALF)
    tables, selects = [], []
    for which in range(2):
        order = first + which + 1
        phase = (order[:, None] * position[None, :]) % POINTS
        angle = phase * (2.0 * math.pi / POINTS)
        both = np.concatenate([np.cos(angle), -np.sin(angle)]) / math.sqrt(POINTS)
        tables.append(np.concatenate(split_two(both)))
        pick = (first + which)[:, None] == np.arange(CHANNELS)[None, :]
        selects.append(np.concatenate([pick, pick]))
    lane = np.arange(4 * LANES)
    device, rest = np.divmod(lane, LANES)
    spectrum, within = np.divmod(rest, IN_DEV)
    target = spectrum * LANES + device * IN_DEV + within
    permute = np.zeros((4 * LANES, 4 * LANES))
    permute[lane, target] = 1.0
    return (
        np.stack(tables).astype(jnp.bfloat16),
        np.stack(selects).astype(jnp.bfloat16),
        permute.astype(jnp.bfloat16),
    )


def transposed_dot(left, right):
    return lax.dot_general(left, right, (((1,), (1,)), ((), ())), preferred_element_type=F32)


def gather_kernel(
    volt_ref, taper_ref, gain_ref, table_hbm, select_ref, permute_hbm, out_ref,
    volts, table, permute, sums, halo_sums, stage, halo_out, halo_in, tiles, other, gathered,
    load_sem, const_sem, halo_sem, swap_send, swap_recv, ring_send, ring_recv,
):
    chan, feed = lax.axis_index("chan"), lax.axis_index("feed")
    core = chan % 2
    parity = (chan // 2) % 2
    column = chan // 4
    high = 2 * feed + parity
    place = column * 2 + core

    def at(where, level):
        level = (level + RING) % RING
        return {"chan": (where // 2) * 4 + (level % 2) * 2 + where % 2, "feed": level // 2}

    def load(half):
        rows = pl.ds(8 * half, 8)
        for index in range(POINTS // LANES):
            source = volt_ref.at[:, rows, pl.ds(index * LANES, LANES)]
            pltpu.make_async_copy(source, volts.at[index, :, rows], load_sem.at[half]).start()

    def loaded(half):
        target = volts.at[:, :, pl.ds(8 * half, 8)]
        pltpu.make_async_copy(target, target, load_sem.at[half]).wait()

    for half in (1, 0):
        load(half)
        if half == 1:
            table_copy = pltpu.make_async_copy(table_hbm, table, const_sem.at[0])
            table_copy.start()
    permute_copy = pltpu.make_async_copy(permute_hbm, permute, const_sem.at[1])
    permute_copy.start()

    barrier = pltpu.get_barrier_semaphore()

    def greet(step, _):
        pl.semaphore_signal(
            barrier, inc=1, device_id=at((place + step) % SOURCES, high), device_id_type=MESH
        )
        return 0

    lax.fori_loop(1, SOURCES, greet, 0)
    for hop in (-2, -1, 1, 2):
        pl.semaphore_signal(barrier, inc=1, device_id=at(place, high + hop), device_id_type=MESH)

    flat = volts.reshape(POINTS // LANES, IN_DEV * SPECS, LANES)

    def block(index, spectrum, step):
        rows = pl.ds(index * 16 * SPECS + spectrum, 16, stride=SPECS)
        return flat[step, rows, :].astype(F32)

    def keep(target, row, lanes, first, second):
        for which, value in enumerate((first - second, first + second)):
            upper = value.astype(BF16)
            lower = (value - upper.astype(F32)).astype(BF16)
            target[which, 0, row, lanes] = upper
            target[which, 1, row, lanes] = lower

    def tapers(lanes):
        return [taper_ref[tap : tap + 1, lanes] for tap in range(TAPS)]

    def lanes_of(step):
        start = pl.multiple_of(step * LANES, LANES)
        return pl.ds(start, LANES), pl.ds(start + HALF, LANES)

    def halo_step(step, _):
        index = step % 2
        here, beyond = lanes_of(step // 2)
        pair = []
        for lanes, tile in ((here, step // 2), (beyond, step // 2 + HALF // LANES)):
            taps = tapers(lanes)
            held = [block(index, SPECS - 3 + back, tile) for back in range(3)]
            pair.append(
                [sum(taps[tap] * held[row + tap] for tap in range(3 - row)) for row in range(3)]
            )
        for row in range(3):
            start = pl.multiple_of(row * IN_DEV + index * 16, 16)
            keep(halo_sums, pl.ds(start, 16), here, pair[0][row], pair[1][row])
        return 0

    def main_step(step, _):
        index = step % 2
        here, beyond = lanes_of(step // 2)
        first_taps, second_taps = tapers(here), tapers(beyond)
        first, second = [], []
        for row in range(SPECS):
            first.append(block(index, row, step // 2))
            second.append(block(index, row, step // 2 + HALF // LANES))
            reach = [tap for tap in range(TAPS) if row - 3 + tap >= 0]
            one = sum(first_taps[tap] * first[row - 3 + tap] for tap in reach)
            two = sum(second_taps[tap] * second[row - 3 + tap] for tap in reach)
            start = pl.multiple_of(row * IN_DEV + index * 16, 16)
            keep(sums, pl.ds(start, 16), here, one, two)
        return 0

    def transform(source, which, rows):
        wide = transposed_dot(table[which], source[which, 0, rows])
        narrow = transposed_dot(table[which, :LANES], source[which, 1, rows])
        return wide[:LANES] + wide[LANES:] + narrow

    halo_sums[:, :, 3 * IN_DEV :] = jnp.zeros((2, 2, IN_DEV, HALF), BF16)
    loaded(1)
    lax.fori_loop(0, 2 * HALF // LANES, halo_step, 0)
    table_copy.wait()
    for which in range(2):
        halo_out[which] = transform(halo_sums, which, pl.ds(0, LANES)).astype(BF16)

    pl.semaphore_wait(barrier, SOURCES - 1 + 4)
    halo_copy = pltpu.make_async_remote_copy(
        src_ref=halo_out, dst_ref=halo_in, send_sem=halo_sem.at[0], recv_sem=halo_sem.at[1],
        device_id=at(place, high + 2), device_id_type=MESH,
    )

    @pl.when(feed < RING // 2 - 1)
    def _():
        halo_copy.start()

    loaded(0)
    lax.fori_loop(0, 2 * HALF // LANES, main_step, 0)

    gain_rows = jnp.concatenate([gain_ref[...].astype(F32).astype(BF16)] * 4, axis=0)

    @pl.when(feed == 0)
    def _():
        halo_in[...] = jnp.zeros_like(halo_in)

    @pl.when(feed > 0)
    def _():
        halo_copy.wait_recv()

    for which in range(2):
        factor = transposed_dot(select_ref[which], gain_rows) * (1.0 / 4096.0)
        for part in range(2):
            lines = pl.ds(part * 2 * LANES, 2 * LANES)
            spectra = transform(sums, which, lines)
            for within in range(2):
                group = part * 2 + within
                value = spectra[:, within * LANES : (within + 1) * LANES]
                if group == 0:
                    value = value + halo_in[which].astype(F32)
                value = value * factor
                for side in range(2):
                    rows = pl.ds(side * 8 + which * 4 + group, 2 * SOURCES, stride=TILE)
                    stage[rows, :] = value[side * 2 * SOURCES : (side + 1) * 2 * SOURCES]
    tiles[...] = stage[...].astype(BF16).reshape(2, SOURCES, TILE, LANES)

    def swap(step, kind, start):
        to = (place + step) % SOURCES
        source = tiles.at[(parity + 1 + kind) % 2, to]
        target = gathered.at[high, place] if kind else other.at[place]
        copy = pltpu.make_async_remote_copy(
            src_ref=source, dst_ref=target, send_sem=swap_send.at[kind], recv_sem=swap_recv.at[kind],
            device_id=at(to, high), device_id_type=MESH,
        )
        copy.start()

    for kind in range(2):

        def swap_step(step, _, kind=kind):
            swap(step, kind, True)
            return 0

        lax.fori_loop(1, SOURCES, swap_step, 0)
        source = tiles.at[(parity + 1 + kind) % 2, place]
        target = gathered.at[high, place] if kind else other.at[place]
        pltpu.make_async_copy(source, target, swap_recv.at[kind]).start()

    def landed(kind):
        whole = gathered.at[high] if kind else other
        pltpu.make_async_copy(whole, whole, swap_recv.at[kind]).wait()

    def ring(slot, chunk):
        up = slot % 2 == 0
        sign = 1 if up else -1
        piece = pl.ds(chunk * PIECE, PIECE)
        kind = slot // 2
        if kind == 0:
            source, origin, hop = other.at[piece], high, sign
        elif kind == 1:
            source, origin, hop = gathered.at[high, piece], high, 2 * sign
        elif kind == 2:
            origin, hop = (high - sign + RING) % RING, 2 * sign
            source = gathered.at[origin, piece]
        else:
            origin, hop = (high - 2 * sign + RING) % RING, 2 * sign
            source = gathered.at[origin, piece]
        return pltpu.make_async_remote_copy(
            src_ref=source, dst_ref=gathered.at[origin, piece],
            send_sem=ring_send.at[slot, chunk], recv_sem=ring_recv.at[slot, chunk],
            device_id=at(place, high + hop), device_id_type=MESH,
        )

    def arrival(slot, chunk):
        sign = 1 if slot % 2 == 0 else -1
        reach = {0: 1, 1: 2, 2: 3, 3: 4}[slot // 2]
        origin = (high - reach * sign + RING) % RING
        target = gathered.at[origin, pl.ds(chunk * PIECE, PIECE)]
        pltpu.make_async_remote_copy(
            src_ref=target, dst_ref=target,
            send_sem=ring_send.at[slot, chunk], recv_sem=ring_recv.at[slot, chunk],
            device_id=at(place, high + 1), device_id_type=MESH,
        ).wait_recv()

    half_chunks = (range(CHUNKS // 2), range(CHUNKS // 2, CHUNKS))
    sent = []

    def send(slot, chunk):
        copy = ring(slot, chunk)
        copy.start()
        sent.append(copy)

    landed(0)
    for chunk in range(CHUNKS):
        send(0, chunk)
        send(1, chunk)
    landed(1)
    for chunk in range(CHUNKS):
        send(2, chunk)
        send(3, chunk)
    for chunk in range(CHUNKS):
        for slot in (0, 1):
            arrival(slot, chunk)
            send(slot + 4, chunk)
    for step in range(CHUNKS):
        for slot in (2, 3):
            arrival(slot, step)
            if step in half_chunks[slot - 2]:
                send(slot + 4, step)
    for chunk in range(CHUNKS):
        for slot in (4, 5):
            arrival(slot, chunk)
    for slot in (6, 7):
        for chunk in half_chunks[slot - 6]:
            arrival(slot, chunk)

    permute_copy.wait()
    for shard in range(RING // 2):
        turned = None
        for side in range(4):
            low, device = divmod(side, 2)
            held = gathered[2 * shard + low].reshape(COLUMNS, 2, TILE, LANES)[:, device]
            term = jnp.dot(
                held.reshape(COLUMNS * TILE, LANES), permute[side * LANES : (side + 1) * LANES],
                preferred_element_type=F32,
            )
            turned = term if turned is None else turned + term
        turned = turned.astype(BF16)
        for spectrum in range(4):
            for where in range(COLUMNS):
                row = (shard * 4 + spectrum) * TILE
                out_ref[row : row + TILE, where * LANES : (where + 1) * LANES] = turned[
                    where * TILE : (where + 1) * TILE, spectrum * LANES : (spectrum + 1) * LANES
                ]

    for kind in range(2):
        some = tiles.at[0, pl.ds(0, SOURCES - 1)]
        pltpu.make_async_copy(some, some, swap_send.at[kind]).wait()
    for copy in sent:
        copy.wait_send()

    @pl.when(feed < RING // 2 - 1)
    def _():
        halo_copy.wait_send()


def correlate_kernel(signal_ref, out_ref, left):
    feed = lax.axis_index("feed")
    rows = out_ref.shape[2]
    depth = signal_ref.shape[0]

    @pl.when(pl.program_id(0) == 0)
    def _():
        own = signal_ref[:, pl.ds(pl.multiple_of(feed * rows, rows), rows)].astype(F32)
        own = own.reshape(depth // TILE, 2, 8, rows)
        swapped = jnp.stack([own[:, 1], -own[:, 0]], axis=1)
        second = lax.broadcasted_iota(jnp.int32, own.shape, 2) >= 4
        for which in range(2):
            for part, value in enumerate((own, swapped)):
                masked = jnp.where(second if which else ~second, value, 0.0)
                left[which, part] = masked.reshape(depth, rows).T.astype(BF16)

    columns = out_ref.shape[3]
    start = pl.multiple_of(pl.program_id(0) * columns, columns)
    right = signal_ref[:, pl.ds(start, columns)]
    for which in range(2):
        for part in range(2):
            summed = jnp.dot(left[which, part], right, preferred_element_type=F32)
            out_ref[which, part] = (summed * (1.0 / 64.0)).astype(BF16)


def on_device(voltages, taper, gains):
    table, select, permute = (jnp.asarray(value) for value in constants())
    inputs = SOURCES * 2 * IN_DEV
    depth = 4 * 4 * TILE
    whole = pl.BlockSpec(memory_space=pltpu.VMEM)
    anywhere = pl.BlockSpec(memory_space=pl.ANY)
    signals = pl.pallas_call(
        gather_kernel,
        out_shape=jax.ShapeDtypeStruct((depth, inputs), BF16),
        in_specs=[anywhere, whole, whole, anywhere, whole, anywhere],
        out_specs=whole,
        scratch_shapes=[
            pltpu.VMEM((POINTS // LANES, IN_DEV, SPECS, LANES), jnp.int32),
            pltpu.VMEM(table.shape, BF16),
            pltpu.VMEM(permute.shape, BF16),
            pltpu.VMEM((2, 2, SPECS * IN_DEV, HALF), BF16),
            pltpu.VMEM((2, 2, LANES, HALF), BF16),
            pltpu.VMEM((2 * SOURCES * TILE, LANES), F32),
            pltpu.VMEM((2, LANES, LANES), BF16),
            pltpu.VMEM((2, LANES, LANES), BF16),
            pltpu.VMEM((2, SOURCES, TILE, LANES), BF16),
            pltpu.VMEM((SOURCES, TILE, LANES), BF16),
            pltpu.VMEM((RING, SOURCES, TILE, LANES), BF16),
            pltpu.SemaphoreType.DMA((2,)),
            pltpu.SemaphoreType.DMA((2,)),
            pltpu.SemaphoreType.DMA((2,)),
            pltpu.SemaphoreType.DMA((2,)),
            pltpu.SemaphoreType.DMA((2,)),
            pltpu.SemaphoreType.DMA((8, CHUNKS)),
            pltpu.SemaphoreType.DMA((8, CHUNKS)),
        ],
        compiler_params=pltpu.CompilerParams(
            collective_id=0, has_side_effects=True, vmem_limit_bytes=48 * 1024 * 1024
        ),
    )(voltages, taper, gains, table, select, permute)
    rows, columns = inputs // 4, 256
    return pl.pallas_call(
        correlate_kernel,
        grid=(inputs // columns,),
        out_shape=jax.ShapeDtypeStruct((2, 2, rows, inputs), BF16),
        in_specs=[pl.BlockSpec((depth, inputs), lambda step: (0, 0))],
        out_specs=pl.BlockSpec((2, 2, rows, columns), lambda step: (0, 0, 0, step)),
        scratch_shapes=[pltpu.VMEM((2, 2, rows, depth), BF16)],
        compiler_params=pltpu.CompilerParams(vmem_limit_bytes=48 * 1024 * 1024),
    )(signals)


def solution(mesh):
    placed = (P("chan", "feed", None), P(), P("chan", None))
    return jax.shard_map(
        on_device,
        mesh=mesh,
        in_specs=placed,
        out_specs=P("chan", None, "feed", None),
        check_vma=False,
    )
```

```python
import functools
import math

import jax
import jax.numpy as jnp
import numpy as np
from jax import lax
from jax.experimental import pallas as pl
from jax.experimental.pallas import tpu as pltpu
from jax.sharding import PartitionSpec as P

MESH = pl.DeviceIdType.MESH
F32, BF16 = jnp.float32, jnp.bfloat16

POINTS = 2048
HALF = POINTS // 2
CHANNELS = 128
IN_DEV = 32
SPECS = 16
TAPS = 4
COLUMNS = 16
RING = 8
SOURCES = 2 * COLUMNS
TILE = 16
LANES = 128
CHUNKS = 2
PIECE = SOURCES // CHUNKS


def tile_channel():
    parity, place = np.divmod(np.arange(2 * SOURCES), SOURCES)
    column, core = np.divmod(place, 2)
    return 2 * (column * 4 + parity * 2 + core)


def split_two(value):
    high = value.astype(jnp.bfloat16)
    low = (value - high.astype(np.float64)).astype(jnp.bfloat16)
    return high, low


def constants():
    first = tile_channel()
    position = np.arange(HALF)
    tables, selects = [], []
    for which in range(2):
        order = first + which + 1
        phase = (order[:, None] * position[None, :]) % POINTS
        angle = phase * (2.0 * math.pi / POINTS)
        both = np.concatenate([np.cos(angle), -np.sin(angle)]) / math.sqrt(POINTS)
        tables.append(np.concatenate(split_two(both)))
        pick = (first + which)[:, None] == np.arange(CHANNELS)[None, :]
        selects.append(np.concatenate([pick, pick]))
    lane = np.arange(4 * LANES)
    device, rest = np.divmod(lane, LANES)
    spectrum, within = np.divmod(rest, IN_DEV)
    target = spectrum * LANES + device * IN_DEV + within
    permute = np.zeros((4 * LANES, 4 * LANES))
    permute[lane, target] = 1.0
    line = np.arange(LANES)
    within = line % TILE
    turns = []
    for which in range(2):
        chosen = (within // 4) % 2 == which
        same = np.diag(np.where(chosen, 1.0 / 64.0, 0.0))
        cross = np.zeros((LANES, LANES))
        cross[line, line ^ 8] = np.where(within < 8, -1.0 / 64.0, 1.0 / 64.0)
        turns += [same, cross * chosen[None, :]]
    return (
        np.stack(tables).astype(jnp.bfloat16),
        np.stack(selects).astype(jnp.bfloat16),
        permute.astype(jnp.bfloat16),
        np.concatenate(turns, axis=1).astype(jnp.bfloat16),
    )


def transposed_dot(left, right):
    return lax.dot_general(left, right, (((1,), (1,)), ((), ())), preferred_element_type=F32)


def gather_kernel(
    volt_hbm, taper_hbm, gain_hbm, table_hbm, select_hbm, permute_hbm, turns_hbm, out_ref, left_ref,
    volts, taper_ref, gain_ref, table, select_ref, permute, turns, sums, halo_sums, stage, halo_out, halo_in, tiles, other, gathered,
    load_sem, const_sem, halo_sem, swap_send, swap_recv, ring_send, ring_recv,
):
    chan, feed = lax.axis_index("chan"), lax.axis_index("feed")
    core = lax.rem(chan, 2)
    parity = lax.rem(lax.div(chan, 2), 2)
    column = lax.div(chan, 4)
    high = 2 * feed + parity
    place = column * 2 + core

    def level_of(level):
        return lax.rem(level + RING, RING)

    def ring_at(hop):
        level = level_of(high + hop)
        return {"chan": column * 4 + lax.rem(level, 2) * 2 + core, "feed": lax.div(level, 2)}

    def plane_at(where):
        return {"chan": lax.div(where, 2) * 4 + parity * 2 + lax.rem(where, 2)}

    def load(half, part):
        some = pl.ds(part * IN_DEV // 2, IN_DEV // 2)
        return pltpu.make_async_copy(
            volt_hbm.at[some, half], volts.at[some, half], load_sem.at[half, part]
        )

    small = (
        (taper_hbm, taper_ref), (table_hbm, table), (gain_hbm, gain_ref), (select_hbm, select_ref),
        (permute_hbm, permute), (turns_hbm, turns),
    )
    copies = [pltpu.make_async_copy(*pair, const_sem.at[n]) for n, pair in enumerate(small)]
    taper_copy, table_copy, gain_copy, select_copy, permute_copy, turns_copy = copies
    taper_copy.start()
    for half in (1, 0):
        for part in range(2):
            load(half, part).start()
        if half == 1:
            table_copy.start()
    for copy in copies[2:]:
        copy.start()

    barrier = pltpu.get_barrier_semaphore()

    def greet(step, _):
        pl.semaphore_signal(
            barrier, inc=1, device_id=plane_at(lax.rem(place + step, SOURCES)), device_id_type=MESH
        )
        return 0

    lax.fori_loop(1, SOURCES, greet, 0)
    for hop in (-2, -1, 1, 2):
        pl.semaphore_signal(barrier, inc=1, device_id=ring_at(hop), device_id_type=MESH)

    flat = volts.reshape(IN_DEV * SPECS * POINTS // LANES, LANES)

    def block(part, spectrum, tile):
        half, line = divmod(spectrum, 8)
        start = (part * IN_DEV + half) * POINTS // LANES * 8 + tile * 8 + line
        return flat[pl.ds(start, 16, stride=SPECS * POINTS // LANES), :].astype(F32)

    def keep(target, row, lanes, first, second):
        for which, value in enumerate((first - second, first + second)):
            upper = value.astype(BF16)
            lower = (value - upper.astype(F32)).astype(BF16)
            target[which, 0, row, lanes] = upper
            target[which, 1, row, lanes] = lower

    def tapers(lanes):
        return [taper_ref[tap : tap + 1, lanes] for tap in range(TAPS)]

    def lanes_of(step):
        start = pl.multiple_of(step * LANES, LANES)
        return pl.ds(start, LANES), pl.ds(start + HALF, LANES)

    def halo_step(step, _, part):
        here, beyond = lanes_of(step)
        pair = []
        for lanes, tile in ((here, step), (beyond, step + HALF // LANES)):
            taps = tapers(lanes)
            held = [block(part, SPECS - 3 + back, tile) for back in range(3)]
            pair.append(
                [sum(taps[tap] * held[row + tap] for tap in range(3 - row)) for row in range(3)]
            )
        for row in range(3):
            keep(halo_sums, pl.ds(row * IN_DEV + part * 16, 16), here, pair[0][row], pair[1][row])
        return 0

    def main_step(step, _, part):
        here, beyond = lanes_of(step)
        first_taps, second_taps = tapers(here), tapers(beyond)
        first, second = [], []
        for row in range(SPECS):
            first.append(block(part, row, step))
            second.append(block(part, row, step + HALF // LANES))
            reach = [tap for tap in range(TAPS) if row - 3 + tap >= 0]
            one = sum(first_taps[tap] * first[row - 3 + tap] for tap in reach)
            two = sum(second_taps[tap] * second[row - 3 + tap] for tap in reach)
            keep(sums, pl.ds(row * IN_DEV + part * 16, 16), here, one, two)
        return 0

    def transform(source, which, rows):
        wide = transposed_dot(table[which], source[which, 0, rows])
        narrow = transposed_dot(table[which, :LANES], source[which, 1, rows])
        return wide[:LANES] + wide[LANES:] + narrow

    halo_sums[:, :, 3 * IN_DEV :] = jnp.zeros((2, 2, IN_DEV, HALF), BF16)
    taper_copy.wait()
    for part in range(2):
        load(1, part).wait()
        lax.fori_loop(0, HALF // LANES, functools.partial(halo_step, part=part), 0)
    table_copy.wait()
    for which in range(2):
        halo_out[which] = transform(halo_sums, which, pl.ds(0, LANES)).astype(BF16)

    pl.semaphore_wait(barrier, SOURCES - 1 + 4)
    halo_copy = pltpu.make_async_remote_copy(
        src_ref=halo_out, dst_ref=halo_in, send_sem=halo_sem.at[0], recv_sem=halo_sem.at[1],
        device_id=ring_at(2), device_id_type=MESH,
    )

    @pl.when(feed < RING // 2 - 1)
    def _():
        halo_copy.start()

    for part in range(2):
        load(0, part).wait()
        lax.fori_loop(0, HALF // LANES, functools.partial(main_step, part=part), 0)

    gain_copy.wait()
    select_copy.wait()
    gain_rows = jnp.concatenate([gain_ref[...].astype(F32).astype(BF16)] * 4, axis=0)

    factors = [transposed_dot(select_ref[which], gain_rows) * (1.0 / 4096.0) for which in range(2)]

    def settle(which, group, value):
        value = value * factors[which]
        for side in range(2):
            rows = pl.ds(side * 8 + which * 4 + group, 2 * SOURCES, stride=TILE)
            stage[rows, :] = value[side * 2 * SOURCES : (side + 1) * 2 * SOURCES]

    firsts = []
    for which in range(2):
        for part in (1, 0):
            spectra = transform(sums, which, pl.ds(part * 2 * LANES, 2 * LANES))
            for within in range(2):
                value = spectra[:, within * LANES : (within + 1) * LANES]
                if part + within == 0:
                    firsts.append(value)
                else:
                    settle(which, part * 2 + within, value)

    @pl.when(feed == 0)
    def _():
        halo_in[...] = jnp.zeros_like(halo_in)

    @pl.when(feed > 0)
    def _():
        halo_copy.wait_recv()

    for which in range(2):
        settle(which, 0, firsts[which] + halo_in[which].astype(F32))
    tiles[...] = stage[...].astype(BF16).reshape(2, SOURCES, TILE, LANES)

    def swap(step, kind, start):
        to = lax.rem(place + step, SOURCES)
        source = tiles.at[lax.rem(parity + 1 + kind, 2), to]
        target = gathered.at[high, place] if kind else other.at[place]
        copy = pltpu.make_async_remote_copy(
            src_ref=source, dst_ref=target, send_sem=swap_send.at[kind], recv_sem=swap_recv.at[kind],
            device_id=plane_at(to), device_id_type=MESH,
        )
        copy.start()

    for kind in range(2):

        def swap_step(step, _, kind=kind):
            swap(step, kind, True)
            return 0

        lax.fori_loop(1, SOURCES, swap_step, 0)
        source = tiles.at[lax.rem(parity + 1 + kind, 2), place]
        target = gathered.at[high, place] if kind else other.at[place]
        pltpu.make_async_copy(source, target, swap_recv.at[kind]).start()

    def landed(kind):
        whole = gathered.at[high] if kind else other
        pltpu.make_async_copy(whole, whole, swap_recv.at[kind]).wait()

    def ring(slot, chunk):
        up = slot % 2 == 0
        sign = 1 if up else -1
        piece = pl.ds(chunk * PIECE, PIECE)
        kind = slot // 2
        if kind == 0:
            source, origin, hop = other.at[piece], high, sign
        elif kind == 1:
            source, origin, hop = gathered.at[high, piece], high, 2 * sign
        elif kind == 2:
            origin, hop = level_of(high - sign), 2 * sign
            source = gathered.at[origin, piece]
        else:
            origin, hop = level_of(high - 2 * sign), 2 * sign
            source = gathered.at[origin, piece]
        return pltpu.make_async_remote_copy(
            src_ref=source, dst_ref=gathered.at[origin, piece],
            send_sem=ring_send.at[slot, chunk], recv_sem=ring_recv.at[slot, chunk],
            device_id=ring_at(hop), device_id_type=MESH,
        )

    def arrival(slot, chunk):
        sign = 1 if slot % 2 == 0 else -1
        reach = {0: 1, 1: 2, 2: 3, 3: 4}[slot // 2]
        origin = level_of(high - reach * sign)
        target = gathered.at[origin, pl.ds(chunk * PIECE, PIECE)]
        pltpu.make_async_remote_copy(
            src_ref=target, dst_ref=target,
            send_sem=ring_send.at[slot, chunk], recv_sem=ring_recv.at[slot, chunk],
            device_id=ring_at(1), device_id_type=MESH,
        ).wait_recv()

    half_chunks = (range(CHUNKS // 2), range(CHUNKS // 2, CHUNKS))
    sent = []

    def send(slot, chunk):
        copy = ring(slot, chunk)
        copy.start()
        sent.append(copy)

    def order(slot, step):
        return step if slot != 3 else CHUNKS - 1 - step

    landed(0)
    send(0, 0)
    send(1, 0)
    landed(1)
    for step in range(CHUNKS):
        for slot in range(4):
            if step or slot >= 2:
                send(slot, order(slot, step))
    for step in range(CHUNKS):
        for slot in range(4):
            chunk = order(slot, step)
            arrival(slot, chunk)
            if slot < 2 or chunk in half_chunks[slot - 2]:
                send(slot + 4, chunk)

    permute_copy.wait()
    turns_copy.wait()

    def turn(order, shard):
        shard = lax.rem(shard + 4, 4)
        turned = None
        for side in range(4):
            low, device = divmod(side, 2)
            held = gathered[2 * shard + low].reshape(COLUMNS, 2, TILE, LANES)[:, device]
            term = jnp.dot(
                held.reshape(COLUMNS * TILE, LANES), permute[side * LANES : (side + 1) * LANES],
                preferred_element_type=F32,
            )
            turned = term if turned is None else turned + term
        turned = turned.astype(BF16)
        for spectrum in range(4):
            for where in range(COLUMNS):
                row = (order * 4 + spectrum) * TILE
                out_ref[row : row + TILE, where * LANES : (where + 1) * LANES] = turned[
                    where * TILE : (where + 1) * TILE, spectrum * LANES : (spectrum + 1) * LANES
                ]

    def prepare(pair):
        rows = left_ref.shape[1]
        own = out_ref[pair * LANES : (pair + 1) * LANES, pl.ds(pl.multiple_of(feed * rows, rows), rows)]
        moved = jnp.dot(own.T, turns[...], preferred_element_type=F32).astype(BF16)
        for index in range(4):
            left_ref[index, :, pair * LANES : (pair + 1) * LANES] = moved[
                :, index * LANES : (index + 1) * LANES
            ]

    turn(0, feed)
    turn(1, feed - 1 + 2 * parity)
    prepare(0)
    for chunk in range(CHUNKS):
        for slot in (4, 5):
            arrival(slot, chunk)
    turn(2, feed + 1 - 2 * parity)
    for slot in (6, 7):
        for chunk in half_chunks[slot - 6]:
            arrival(slot, chunk)
    turn(3, feed + 2)
    prepare(1)
    for kind in range(2):
        some = tiles.at[0, pl.ds(0, SOURCES - 1)]
        pltpu.make_async_copy(some, some, swap_send.at[kind]).wait()
    for copy in sent:
        copy.wait_send()

    @pl.when(feed < RING // 2 - 1)
    def _():
        halo_copy.wait_send()


def correlate_kernel(signal_ref, left_ref, out_hbm, whole, sem):
    columns = 512
    count = whole.shape[3] // columns
    copies = []
    for index in range(4 * count):
        which, part, block = index // (2 * count), index // count % 2, index % count
        some = pl.ds(block * columns, columns)
        summed = jnp.dot(left_ref[2 * which + part], signal_ref[:, some], preferred_element_type=F32)
        whole[which, part, :, some] = summed.astype(BF16)
        copy = pltpu.make_async_copy(
            whole.at[which, part, :, some], out_hbm.at[which, part, :, some], sem.at[index]
        )
        copy.start()
        copies.append(copy)
    for copy in copies:
        copy.wait()


def on_device(voltages, taper, gains):
    table, select, permute, turns = (jnp.asarray(value) for value in constants())
    laid = voltages.reshape(IN_DEV, 2, 8, POINTS // LANES, LANES).transpose(0, 1, 3, 2, 4)
    operands = (laid, taper, gains, table, select, permute, turns)
    inputs = SOURCES * 2 * IN_DEV
    rows = inputs // 4
    depth = 4 * 4 * TILE
    whole = pl.BlockSpec(memory_space=pltpu.VMEM)
    signals, left = pl.pallas_call(
        gather_kernel,
        out_shape=(
            jax.ShapeDtypeStruct((depth, inputs), BF16),
            jax.ShapeDtypeStruct((4, rows, depth), BF16),
        ),
        in_specs=[pl.BlockSpec(memory_space=pl.ANY)] * len(operands),
        out_specs=(whole, whole),
        scratch_shapes=[
            pltpu.VMEM(laid.shape, jnp.int32),
            pltpu.VMEM(taper.shape, F32),
            pltpu.VMEM(gains.shape, jnp.int32),
            pltpu.VMEM(table.shape, BF16),
            pltpu.VMEM(select.shape, BF16),
            pltpu.VMEM(permute.shape, BF16),
            pltpu.VMEM(turns.shape, BF16),
            pltpu.VMEM((2, 2, SPECS * IN_DEV, HALF), BF16),
            pltpu.VMEM((2, 2, LANES, HALF), BF16),
            pltpu.VMEM((2 * SOURCES * TILE, LANES), F32),
            pltpu.VMEM((2, LANES, LANES), BF16),
            pltpu.VMEM((2, LANES, LANES), BF16),
            pltpu.VMEM((2, SOURCES, TILE, LANES), BF16),
            pltpu.VMEM((SOURCES, TILE, LANES), BF16),
            pltpu.VMEM((RING, SOURCES, TILE, LANES), BF16),
            pltpu.SemaphoreType.DMA((2, 2)),
            pltpu.SemaphoreType.DMA((len(operands) - 1,)),
            pltpu.SemaphoreType.DMA((2,)),
            pltpu.SemaphoreType.DMA((2,)),
            pltpu.SemaphoreType.DMA((2,)),
            pltpu.SemaphoreType.DMA((8, CHUNKS)),
            pltpu.SemaphoreType.DMA((8, CHUNKS)),
        ],
        compiler_params=pltpu.CompilerParams(
            collective_id=0, has_side_effects=True, vmem_limit_bytes=48 * 1024 * 1024
        ),
    )(*(pltpu.with_memory_space_constraint(value, pltpu.HBM) for value in operands))
    return pl.pallas_call(
        correlate_kernel,
        out_shape=jax.ShapeDtypeStruct((2, 2, rows, inputs), BF16),
        in_specs=[whole, whole],
        out_specs=pl.BlockSpec(memory_space=pl.ANY),
        scratch_shapes=[pltpu.VMEM((2, 2, rows, inputs), BF16), pltpu.SemaphoreType.DMA((16,))],
        compiler_params=pltpu.CompilerParams(vmem_limit_bytes=32 * 1024 * 1024),
    )(signals, left)


def solution(mesh):
    placed = (P("chan", "feed", None), P(), P("chan", None))
    return jax.shard_map(
        on_device,
        mesh=mesh,
        in_specs=placed,
        out_specs=P("chan", None, "feed", None),
        check_vma=False,
    )
```

```python
import functools
import math

import jax
import jax.numpy as jnp
import numpy as np
from jax import lax
from jax.experimental import pallas as pl
from jax.experimental.pallas import tpu as pltpu
from jax.sharding import PartitionSpec as P

MESH = pl.DeviceIdType.MESH
F32, BF16 = jnp.float32, jnp.bfloat16

POINTS = 2048
HALF = POINTS // 2
CHANNELS = 128
IN_DEV = 32
SPECS = 16
TAPS = 4
COLUMNS = 16
RING = 8
SOURCES = 2 * COLUMNS
TILE = 16
LANES = 128
ROW = 8
ROWS = SOURCES // ROW
PITCH = SPECS * POINTS // LANES + 8


def tile_channel():
    parity, place = np.divmod(np.arange(2 * SOURCES), SOURCES)
    column, core = np.divmod(place, 2)
    return 2 * (column * 4 + parity * 2 + core)


def split_two(value):
    high = value.astype(jnp.bfloat16)
    low = (value - high.astype(np.float64)).astype(jnp.bfloat16)
    return high, low


def constants():
    first = tile_channel()
    position = np.arange(HALF)
    tables, selects = [], []
    for which in range(2):
        order = first + which + 1
        phase = (order[:, None] * position[None, :]) % POINTS
        angle = phase * (2.0 * math.pi / POINTS)
        both = np.concatenate([np.cos(angle), -np.sin(angle)]) / math.sqrt(POINTS)
        tables.append(np.concatenate(split_two(both)))
        pick = (first + which)[:, None] == np.arange(CHANNELS)[None, :]
        selects.append(np.concatenate([pick, pick]))
    lane = np.arange(4 * LANES)
    device, rest = np.divmod(lane, LANES)
    spectrum, within = np.divmod(rest, IN_DEV)
    target = spectrum * LANES + device * IN_DEV + within
    permute = np.zeros((4 * LANES, 4 * LANES))
    permute[lane, target] = 1.0
    line = np.arange(LANES)
    within = line % TILE
    turns = []
    for which in range(2):
        chosen = (within // 4) % 2 == which
        same = np.diag(np.where(chosen, 1.0 / 64.0, 0.0))
        cross = np.zeros((LANES, LANES))
        cross[line, line ^ 8] = np.where(within < 8, -1.0 / 64.0, 1.0 / 64.0)
        turns += [same, cross * chosen[None, :]]
    return (
        np.stack(tables).astype(jnp.bfloat16),
        np.stack(selects).astype(jnp.bfloat16),
        permute.astype(jnp.bfloat16),
        np.concatenate(turns, axis=1).astype(jnp.bfloat16),
    )


def transposed_dot(left, right):
    return lax.dot_general(left, right, (((1,), (1,)), ((), ())), preferred_element_type=F32)


def gather_kernel(
    volt_hbm, taper_hbm, gain_hbm, table_hbm, select_hbm, permute_hbm, turns_hbm, out_ref, left_ref,
    volts, taper_ref, gain_ref, table, select_ref, permute, turns, sums, halo_sums, stage, halo_out, halo_in, tiles, other, passing, gathered,
    load_sem, const_sem, halo_sem, swap_send, swap_recv, ring_send, ring_recv,
):
    chan, feed = lax.axis_index("chan"), lax.axis_index("feed")
    core = lax.rem(chan, 2)
    parity = lax.rem(lax.div(chan, 2), 2)
    column = lax.div(chan, 4)
    high = 2 * feed + parity
    place = column * 2 + core
    line = lax.div(place, ROW)
    near = pl.ds(pl.multiple_of(line * ROW, ROW), ROW)

    def level_of(level):
        return lax.rem(level + RING, RING)

    def ring_at(hop):
        level = level_of(high + hop)
        return {"chan": column * 4 + lax.rem(level, 2) * 2 + core, "feed": lax.div(level, 2)}

    def plane_at(where):
        return {"chan": lax.div(where, 2) * 4 + parity * 2 + lax.rem(where, 2)}

    def load(half, part):
        some = pl.ds(part * IN_DEV // 2, IN_DEV // 2)
        lines = pl.ds(half * POINTS // LANES * 8, POINTS // LANES * 8)
        return pltpu.make_async_copy(
            volt_hbm.at[some, lines], volts.at[some, lines], load_sem.at[half, part]
        )

    small = (
        (taper_hbm, taper_ref), (table_hbm, table), (gain_hbm, gain_ref), (select_hbm, select_ref),
        (permute_hbm, permute), (turns_hbm, turns),
    )
    copies = [pltpu.make_async_copy(*pair, const_sem.at[n]) for n, pair in enumerate(small)]
    taper_copy, table_copy, gain_copy, select_copy, permute_copy, turns_copy = copies
    taper_copy.start()
    for half in (1, 0):
        for part in range(2):
            load(half, part).start()
        if half == 1:
            table_copy.start()
    for copy in copies[2:]:
        copy.start()

    barrier = pltpu.get_barrier_semaphore()

    def greet(step, _):
        pl.semaphore_signal(
            barrier, inc=1, device_id=plane_at(lax.rem(place + step, SOURCES)), device_id_type=MESH
        )
        return 0

    lax.fori_loop(1, SOURCES, greet, 0)
    for hop in (-2, -1, 1, 2):
        pl.semaphore_signal(barrier, inc=1, device_id=ring_at(hop), device_id_type=MESH)

    flat = volts.reshape(IN_DEV * PITCH, LANES)

    def block(part, spectrum, tile):
        half, line = divmod(spectrum, 8)
        start = part * 16 * PITCH + half * POINTS // LANES * 8 + tile * 8 + line
        return flat[pl.ds(start, 16, stride=PITCH), :].astype(F32)

    def keep(target, row, lanes, first, second):
        for which, value in enumerate((first - second, first + second)):
            upper = value.astype(BF16)
            lower = (value - upper.astype(F32)).astype(BF16)
            target[which, 0, row, lanes] = upper
            target[which, 1, row, lanes] = lower

    def tapers(lanes):
        return [taper_ref[tap : tap + 1, lanes] for tap in range(TAPS)]

    def lanes_of(step):
        start = pl.multiple_of(step * LANES, LANES)
        return pl.ds(start, LANES), pl.ds(start + HALF, LANES)

    def halo_step(step, _, part):
        here, beyond = lanes_of(step)
        pair = []
        for lanes, tile in ((here, step), (beyond, step + HALF // LANES)):
            taps = tapers(lanes)
            held = [block(part, SPECS - 3 + back, tile) for back in range(3)]
            pair.append(
                [sum(taps[tap] * held[row + tap] for tap in range(3 - row)) for row in range(3)]
            )
        for row in range(3):
            keep(halo_sums, pl.ds(row * IN_DEV + part * 16, 16), here, pair[0][row], pair[1][row])
        return 0

    def main_step(step, _, part):
        here, beyond = lanes_of(step)
        first_taps, second_taps = tapers(here), tapers(beyond)
        first, second = [], []
        for row in range(SPECS):
            first.append(block(part, row, step))
            second.append(block(part, row, step + HALF // LANES))
            reach = [tap for tap in range(TAPS) if row - 3 + tap >= 0]
            one = sum(first_taps[tap] * first[row - 3 + tap] for tap in reach)
            two = sum(second_taps[tap] * second[row - 3 + tap] for tap in reach)
            keep(sums, pl.ds(row * IN_DEV + part * 16, 16), here, one, two)
        return 0

    def transform(source, which, rows):
        wide = transposed_dot(table[which], source[which, 0, rows])
        narrow = transposed_dot(table[which, :LANES], source[which, 1, rows])
        return wide[:LANES] + wide[LANES:] + narrow

    halo_sums[:, :, 3 * IN_DEV :] = jnp.zeros((2, 2, IN_DEV, HALF), BF16)
    taper_copy.wait()
    for part in range(2):
        load(1, part).wait()
        lax.fori_loop(0, HALF // LANES, functools.partial(halo_step, part=part), 0)
    table_copy.wait()
    for which in range(2):
        halo_out[which] = transform(halo_sums, which, pl.ds(0, LANES)).astype(BF16)

    pl.semaphore_wait(barrier, SOURCES - 1 + 4)
    halo_copy = pltpu.make_async_remote_copy(
        src_ref=halo_out, dst_ref=halo_in, send_sem=halo_sem.at[0], recv_sem=halo_sem.at[1],
        device_id=ring_at(2), device_id_type=MESH,
    )

    @pl.when(feed < RING // 2 - 1)
    def _():
        halo_copy.start()

    for part in range(2):
        load(0, part).wait()
        lax.fori_loop(0, HALF // LANES, functools.partial(main_step, part=part), 0)

    gain_copy.wait()
    select_copy.wait()
    gain_rows = jnp.concatenate([gain_ref[...].astype(F32).astype(BF16)] * 4, axis=0)

    factors = [transposed_dot(select_ref[which], gain_rows) * (1.0 / 4096.0) for which in range(2)]

    def settle(which, group, value):
        value = value * factors[which]
        for side in range(2):
            rows = pl.ds(side * 8 + which * 4 + group, 2 * SOURCES, stride=TILE)
            stage[rows, :] = value[side * 2 * SOURCES : (side + 1) * 2 * SOURCES]

    firsts = []
    for which in range(2):
        for part in (1, 0):
            spectra = transform(sums, which, pl.ds(part * 2 * LANES, 2 * LANES))
            for within in range(2):
                value = spectra[:, within * LANES : (within + 1) * LANES]
                if part + within == 0:
                    firsts.append(value)
                else:
                    settle(which, part * 2 + within, value)

    @pl.when(feed == 0)
    def _():
        halo_in[...] = jnp.zeros_like(halo_in)

    @pl.when(feed > 0)
    def _():
        halo_copy.wait_recv()

    for which in range(2):
        settle(which, 0, firsts[which] + halo_in[which].astype(F32))
    tiles[...] = stage[...].astype(BF16).reshape(2, SOURCES, TILE, LANES)

    def push(source, target, send_sem, recv_sem, device):
        return pltpu.make_async_remote_copy(
            src_ref=source, dst_ref=target, send_sem=send_sem, recv_sem=recv_sem,
            device_id=device, device_id_type=MESH,
        )

    def far_row(step):
        return lax.rem(line + step, ROWS) * ROW

    def held(step, origin, start=0, count=ROW):
        if step == 0:
            return passing.at[origin, pl.ds(start, count)]
        return gathered.at[origin, pl.ds(far_row(step) + start, count)]

    def part_of(slot):
        return {6: (0, ROW // 2), 7: (ROW // 2, ROW // 2)}.get(slot, (0, ROW))

    def ring(slot, step):
        sign = 1 if slot % 2 == 0 else -1
        kind = slot // 2
        start, count = part_of(slot)
        hop = sign if kind == 0 else 2 * sign
        origin = level_of(high - {0: 0, 1: 0, 2: 1, 3: 2}[kind] * sign)
        if kind >= 2:
            source = held(step, origin, start, count)
        elif step == 0:
            source = tiles.at[lax.rem(parity + 1 + kind, 2), near]
        elif kind == 0:
            source = other.at[pl.ds(far_row(step), ROW)]
        else:
            source = gathered.at[high, pl.ds(far_row(step), ROW)]
        return push(
            source, held(step, origin, start, count),
            ring_send.at[slot, step], ring_recv.at[slot, step], ring_at(hop),
        )

    def arrival(slot, step):
        sign = 1 if slot % 2 == 0 else -1
        reach = {0: 1, 1: 2, 2: 3, 3: 4}[slot // 2]
        target = held(step, level_of(high - reach * sign), *part_of(slot))
        push(target, target, ring_send.at[slot, step], ring_recv.at[slot, step], ring_at(1)).wait_recv()

    def send(slot, step):
        ring(slot, step).start()

    def hand_on(step):
        for slot in range(4):
            arrival(slot, step)
            send(slot + 4, step)

    for slot in range(4):
        send(slot, 0)

    for kind in range(2):

        def swap_step(step, _, kind=kind):
            to = lax.rem((line + 1) * ROW + step, SOURCES)
            source = tiles.at[lax.rem(parity + 1 + kind, 2), to]
            target = gathered.at[high, place] if kind else other.at[place]
            arrives = swap_recv.at[kind, ROWS - 1 - lax.div(step, ROW)]
            push(source, target, swap_send.at[kind], arrives, plane_at(to)).start()
            return 0

        lax.fori_loop(0, SOURCES - ROW, swap_step, 0)

    def landed(kind, step):
        some = pl.ds(far_row(step), ROW)
        whole = gathered.at[high, some] if kind else other.at[some]
        pltpu.make_async_copy(whole, whole, swap_recv.at[kind, step]).wait()

    def spread():
        for slot in range(4, 8):
            arrival(slot, 0)
        own = pltpu.make_async_copy(tiles.at[parity, near], passing.at[high], swap_recv.at[0, 0])
        own.start()
        own.wait()

        def row_step(step, _):
            index = lax.rem(place + step, ROW)
            push(
                passing.at[:, index], gathered.at[:, place],
                swap_send.at[2], swap_recv.at[1, 0], plane_at(line * ROW + index),
            ).start()
            return 0

        lax.fori_loop(1, ROW, row_step, 0)
        pltpu.make_async_copy(
            passing.at[:, lax.rem(place, ROW)], gathered.at[:, place], swap_recv.at[1, 0]
        ).start()

    hand_on(0)
    for kind in range(2):
        for step in (1, 2):
            landed(kind, step)
            send(2 * kind, step)
            send(2 * kind + 1, step)
    spread()
    for kind in range(2):
        for step in (3,):
            landed(kind, step)
            send(2 * kind, step)
            send(2 * kind + 1, step)
    hand_on(1)
    hand_on(2)
    hand_on(3)
    pltpu.make_async_copy(gathered.at[:, near], gathered.at[:, near], swap_recv.at[1, 0]).wait()

    permute_copy.wait()
    turns_copy.wait()

    def turn(order, shard):
        shard = lax.rem(shard + 4, 4)
        turned = None
        for side in range(4):
            low, device = divmod(side, 2)
            held = gathered[2 * shard + low].reshape(COLUMNS, 2, TILE, LANES)[:, device]
            term = jnp.dot(
                held.reshape(COLUMNS * TILE, LANES), permute[side * LANES : (side + 1) * LANES],
                preferred_element_type=F32,
            )
            turned = term if turned is None else turned + term
        turned = turned.astype(BF16)
        for spectrum in range(4):
            for where in range(COLUMNS):
                row = (order * 4 + spectrum) * TILE
                out_ref[row : row + TILE, where * LANES : (where + 1) * LANES] = turned[
                    where * TILE : (where + 1) * TILE, spectrum * LANES : (spectrum + 1) * LANES
                ]

    def prepare(pair):
        rows = left_ref.shape[1]
        own = out_ref[pair * LANES : (pair + 1) * LANES, pl.ds(pl.multiple_of(feed * rows, rows), rows)]
        moved = jnp.dot(own.T, turns[...], preferred_element_type=F32).astype(BF16)
        for index in range(4):
            left_ref[index, :, pair * LANES : (pair + 1) * LANES] = moved[
                :, index * LANES : (index + 1) * LANES
            ]

    turn(0, feed)
    turn(1, feed - 1 + 2 * parity)
    prepare(0)
    for step in range(1, ROWS):
        arrival(4, step)
        arrival(5, step)
    turn(2, feed + 1 - 2 * parity)
    for step in range(1, ROWS):
        arrival(6, step)
        arrival(7, step)
    turn(3, feed + 2)
    prepare(1)
    for kind in range(2):
        some = tiles.at[0, pl.ds(0, SOURCES - ROW)]
        pltpu.make_async_copy(some, some, swap_send.at[kind]).wait()
    some = passing.at[:, pl.ds(0, ROW - 1)]
    pltpu.make_async_copy(some, some, swap_send.at[2]).wait()
    for slot in range(8):
        for step in range(ROWS):
            ring(slot, step).wait_send()

    @pl.when(feed < RING // 2 - 1)
    def _():
        halo_copy.wait_send()


def correlate_kernel(signal_ref, left_ref, out_hbm, whole, sem):
    columns = 512
    count = whole.shape[3] // columns
    copies = []
    for index in range(4 * count):
        which, part, block = index // (2 * count), index // count % 2, index % count
        some = pl.ds(block * columns, columns)
        summed = jnp.dot(left_ref[2 * which + part], signal_ref[:, some], preferred_element_type=F32)
        whole[which, part, :, some] = summed.astype(BF16)
        copy = pltpu.make_async_copy(
            whole.at[which, part, :, some], out_hbm.at[which, part, :, some], sem.at[index]
        )
        copy.start()
        copies.append(copy)
    for copy in copies:
        copy.wait()


def on_device(voltages, taper, gains):
    table, select, permute, turns = (jnp.asarray(value) for value in constants())
    laid = voltages.reshape(IN_DEV, 2, 8, POINTS // LANES, LANES).transpose(0, 1, 3, 2, 4)
    laid = laid.reshape(IN_DEV, SPECS * POINTS // LANES, LANES)
    operands = (laid, taper, gains, table, select, permute, turns)
    inputs = SOURCES * 2 * IN_DEV
    rows = inputs // 4
    depth = 4 * 4 * TILE
    whole = pl.BlockSpec(memory_space=pltpu.VMEM)
    signals, left = pl.pallas_call(
        gather_kernel,
        out_shape=(
            jax.ShapeDtypeStruct((depth, inputs), BF16),
            jax.ShapeDtypeStruct((4, rows, depth), BF16),
        ),
        in_specs=[pl.BlockSpec(memory_space=pl.ANY)] * len(operands),
        out_specs=(whole, whole),
        scratch_shapes=[
            pltpu.VMEM((IN_DEV, PITCH, LANES), jnp.int32),
            pltpu.VMEM(taper.shape, F32),
            pltpu.VMEM(gains.shape, jnp.int32),
            pltpu.VMEM(table.shape, BF16),
            pltpu.VMEM(select.shape, BF16),
            pltpu.VMEM(permute.shape, BF16),
            pltpu.VMEM(turns.shape, BF16),
            pltpu.VMEM((2, 2, SPECS * IN_DEV, HALF), BF16),
            pltpu.VMEM((2, 2, LANES, HALF), BF16),
            pltpu.VMEM((2 * SOURCES * TILE, LANES), F32),
            pltpu.VMEM((2, LANES, LANES), BF16),
            pltpu.VMEM((2, LANES, LANES), BF16),
            pltpu.VMEM((2, SOURCES, TILE, LANES), BF16),
            pltpu.VMEM((SOURCES, TILE, LANES), BF16),
            pltpu.VMEM((RING, ROW, TILE, LANES), BF16),
            pltpu.VMEM((RING, SOURCES, TILE, LANES), BF16),
            pltpu.SemaphoreType.DMA((2, 2)),
            pltpu.SemaphoreType.DMA((len(operands) - 1,)),
            pltpu.SemaphoreType.DMA((2,)),
            pltpu.SemaphoreType.DMA((3,)),
            pltpu.SemaphoreType.DMA((2, ROWS)),
            pltpu.SemaphoreType.DMA((8, ROWS)),
            pltpu.SemaphoreType.DMA((8, ROWS)),
        ],
        compiler_params=pltpu.CompilerParams(
            collective_id=0, has_side_effects=True, vmem_limit_bytes=48 * 1024 * 1024
        ),
    )(*(pltpu.with_memory_space_constraint(value, pltpu.HBM) for value in operands))
    return pl.pallas_call(
        correlate_kernel,
        out_shape=jax.ShapeDtypeStruct((2, 2, rows, inputs), BF16),
        in_specs=[whole, whole],
        out_specs=pl.BlockSpec(memory_space=pl.ANY),
        scratch_shapes=[pltpu.VMEM((2, 2, rows, inputs), BF16), pltpu.SemaphoreType.DMA((16,))],
        compiler_params=pltpu.CompilerParams(vmem_limit_bytes=32 * 1024 * 1024),
    )(signals, left)


def solution(mesh):
    placed = (P("chan", "feed", None), P(), P("chan", None))
    return jax.shard_map(
        on_device,
        mesh=mesh,
        in_specs=placed,
        out_specs=P("chan", None, "feed", None),
        check_vma=False,
    )
```

```python
import functools
import math

import jax
import jax.numpy as jnp
import numpy as np
from jax import lax
from jax.experimental import pallas as pl
from jax.experimental.pallas import tpu as pltpu
from jax.sharding import PartitionSpec as P

MESH = pl.DeviceIdType.MESH
F32, BF16 = jnp.float32, jnp.bfloat16

POINTS = 2048
HALF = POINTS // 2
CHANNELS = 128
IN_DEV = 32
SPECS = 16
TAPS = 4
COLUMNS = 16
RING = 8
SOURCES = 2 * COLUMNS
TILE = 16
LANES = 128
ROW = 8
ROWS = SOURCES // ROW
NEAR = 2
PITCH = SPECS * POINTS // LANES + 8


def tile_channel():
    parity, place = np.divmod(np.arange(2 * SOURCES), SOURCES)
    column, core = np.divmod(place, 2)
    return 2 * (column * 4 + parity * 2 + core)


def split_two(value):
    high = value.astype(jnp.bfloat16)
    low = (value - high.astype(np.float64)).astype(jnp.bfloat16)
    return high, low


def constants():
    first = tile_channel()
    position = np.arange(HALF)
    tables, selects = [], []
    for which in range(2):
        order = first + which + 1
        phase = (order[:, None] * position[None, :]) % POINTS
        angle = phase * (2.0 * math.pi / POINTS)
        both = np.concatenate([np.cos(angle), -np.sin(angle)]) / math.sqrt(POINTS)
        tables.append(np.concatenate(split_two(both)))
        pick = (first + which)[:, None] == np.arange(CHANNELS)[None, :]
        selects.append(np.concatenate([pick, pick]))
    lane = np.arange(4 * LANES)
    device, rest = np.divmod(lane, LANES)
    spectrum, within = np.divmod(rest, IN_DEV)
    target = spectrum * LANES + device * IN_DEV + within
    permute = np.zeros((4 * LANES, 4 * LANES))
    permute[lane, target] = 1.0
    line = np.arange(LANES)
    within = line % TILE
    turns = []
    for which in range(2):
        chosen = (within // 4) % 2 == which
        same = np.diag(np.where(chosen, 1.0 / 64.0, 0.0))
        cross = np.zeros((LANES, LANES))
        cross[line, line ^ 8] = np.where(within < 8, -1.0 / 64.0, 1.0 / 64.0)
        turns += [same, cross * chosen[None, :]]
    return (
        np.stack(tables).astype(jnp.bfloat16),
        np.stack(selects).astype(jnp.bfloat16),
        permute.astype(jnp.bfloat16),
        np.concatenate(turns, axis=1).astype(jnp.bfloat16),
    )


def transposed_dot(left, right):
    return lax.dot_general(left, right, (((1,), (1,)), ((), ())), preferred_element_type=F32)


def gather_kernel(
    volt_hbm, taper_hbm, gain_hbm, table_hbm, select_hbm, permute_hbm, turns_hbm, out_ref, left_ref,
    volts, taper_ref, gain_ref, table, select_ref, permute, turns, sums, halo_sums, factors, stage, halo_out, halo_in, tiles, other, passing, gathered,
    load_sem, const_sem, halo_sem, swap_send, swap_recv, spread_recv, ring_send, ring_recv,
):
    chan, feed = lax.axis_index("chan"), lax.axis_index("feed")
    core = lax.rem(chan, 2)
    parity = lax.rem(lax.div(chan, 2), 2)
    column = lax.div(chan, 4)
    high = 2 * feed + parity
    place = column * 2 + core
    line = lax.div(place, ROW)

    def level_of(level):
        return lax.rem(level + RING, RING)

    def ring_at(hop):
        level = level_of(high + hop)
        return {"chan": column * 4 + lax.rem(level, 2) * 2 + core, "feed": lax.div(level, 2)}

    def plane_at(where):
        return {"chan": lax.div(where, 2) * 4 + parity * 2 + lax.rem(where, 2)}

    def load(half, part):
        some = pl.ds(part * IN_DEV // 2, IN_DEV // 2)
        lines = pl.ds(half * POINTS // LANES * 8, POINTS // LANES * 8)
        return pltpu.make_async_copy(
            volt_hbm.at[some, lines], volts.at[some, lines], load_sem.at[half, part]
        )

    small = (
        (taper_hbm, taper_ref), (table_hbm, table), (gain_hbm, gain_ref), (select_hbm, select_ref),
        (permute_hbm, permute), (turns_hbm, turns),
    )
    copies = [pltpu.make_async_copy(*pair, const_sem.at[n]) for n, pair in enumerate(small)]
    taper_copy, table_copy, gain_copy, select_copy, permute_copy, turns_copy = copies
    for copy in (taper_copy, gain_copy, select_copy):
        copy.start()
    for half in (1, 0):
        for part in range(2):
            load(half, part).start()
        if half == 1:
            table_copy.start()
    permute_copy.start()
    turns_copy.start()

    barrier = pltpu.get_barrier_semaphore()

    def greet(step, _):
        pl.semaphore_signal(
            barrier, inc=1, device_id=plane_at(lax.rem(place + step, SOURCES)), device_id_type=MESH
        )
        return 0

    lax.fori_loop(1, SOURCES, greet, 0)
    for hop in (-2, -1, 1, 2):
        pl.semaphore_signal(barrier, inc=1, device_id=ring_at(hop), device_id_type=MESH)

    flat = volts.reshape(IN_DEV * PITCH, LANES)

    def block(part, spectrum, tile):
        half, line = divmod(spectrum, 8)
        start = part * 16 * PITCH + half * POINTS // LANES * 8 + tile * 8 + line
        return flat[pl.ds(start, 16, stride=PITCH), :].astype(F32)

    def keep(target, row, lanes, first, second):
        for which, value in enumerate((first - second, first + second)):
            upper = value.astype(BF16)
            lower = (value - upper.astype(F32)).astype(BF16)
            target[which, 0, row, lanes] = upper
            target[which, 1, row, lanes] = lower

    def tapers(lanes):
        return [taper_ref[tap : tap + 1, lanes] for tap in range(TAPS)]

    def lanes_of(step):
        start = pl.multiple_of(step * LANES, LANES)
        return pl.ds(start, LANES), pl.ds(start + HALF, LANES)

    def halo_step(step, _, part):
        here, beyond = lanes_of(step)
        pair = []
        for lanes, tile in ((here, step), (beyond, step + HALF // LANES)):
            taps = tapers(lanes)
            held = [block(part, SPECS - 3 + back, tile) for back in range(3)]
            pair.append(
                [sum(taps[tap] * held[row + tap] for tap in range(3 - row)) for row in range(3)]
            )
        for row in range(3):
            keep(halo_sums, pl.ds(row * IN_DEV + part * 16, 16), here, pair[0][row], pair[1][row])
        return 0

    def main_step(step, _, part):
        here, beyond = lanes_of(step)
        first_taps, second_taps = tapers(here), tapers(beyond)
        first, second = [], []
        for row in range(SPECS):
            first.append(block(part, row, step))
            second.append(block(part, row, step + HALF // LANES))
            reach = [tap for tap in range(TAPS) if row - 3 + tap >= 0]
            one = sum(first_taps[tap] * first[row - 3 + tap] for tap in reach)
            two = sum(second_taps[tap] * second[row - 3 + tap] for tap in reach)
            keep(sums, pl.ds(row * IN_DEV + part * 16, 16), here, one, two)
        return 0

    def transform(source, which, rows):
        wide = transposed_dot(table[which], source[which, 0, rows])
        narrow = transposed_dot(table[which, :LANES], source[which, 1, rows])
        return wide[:LANES] + wide[LANES:] + narrow

    halo_sums[:, :, 3 * IN_DEV :] = jnp.zeros((2, 2, IN_DEV, HALF), BF16)
    gain_copy.wait()
    select_copy.wait()
    gain_rows = jnp.concatenate([gain_ref[...].astype(F32).astype(BF16)] * 4, axis=0)

    for which in range(2):
        factors[which] = transposed_dot(select_ref[which], gain_rows) * (1.0 / 4096.0)
    taper_copy.wait()
    for part in range(2):
        load(1, part).wait()
        lax.fori_loop(0, HALF // LANES, functools.partial(halo_step, part=part), 0)
    table_copy.wait()
    for which in range(2):
        halo_out[which] = transform(halo_sums, which, pl.ds(0, LANES)).astype(BF16)

    pl.semaphore_wait(barrier, SOURCES - 1 + 4)
    halo_copy = pltpu.make_async_remote_copy(
        src_ref=halo_out, dst_ref=halo_in, send_sem=halo_sem.at[0], recv_sem=halo_sem.at[1],
        device_id=ring_at(2), device_id_type=MESH,
    )

    @pl.when(feed < RING // 2 - 1)
    def _():
        halo_copy.start()

    for part in range(2):
        load(0, part).wait()
        lax.fori_loop(0, HALF // LANES, functools.partial(main_step, part=part), 0)

    def settle(which, group, value):
        value = value * factors[which]
        for side in range(2):
            rows = pl.ds(side * 8 + which * 4 + group, 2 * SOURCES, stride=TILE)
            stage[rows, :] = value[side * 2 * SOURCES : (side + 1) * 2 * SOURCES]

    firsts = []
    for which in range(2):
        for part in (1, 0):
            spectra = transform(sums, which, pl.ds(part * 2 * LANES, 2 * LANES))
            for within in range(2):
                value = spectra[:, within * LANES : (within + 1) * LANES]
                if part + within == 0:
                    firsts.append(value)
                else:
                    settle(which, part * 2 + within, value)

    @pl.when(feed == 0)
    def _():
        halo_in[...] = jnp.zeros_like(halo_in)

    @pl.when(feed > 0)
    def _():
        halo_copy.wait_recv()

    for which in range(2):
        settle(which, 0, firsts[which] + halo_in[which].astype(F32))
    tiles[...] = stage[...].astype(BF16).reshape(2, SOURCES, TILE, LANES)

    def push(source, target, send_sem, recv_sem, device):
        return pltpu.make_async_remote_copy(
            src_ref=source, dst_ref=target, send_sem=send_sem, recv_sem=recv_sem,
            device_id=device, device_id_type=MESH,
        )

    def row_at(offset):
        return lax.rem(line + offset + ROWS, ROWS) * ROW

    def far_row(step):
        return row_at(step - NEAR + 1)

    def held(step, origin, start=0, count=ROW):
        if step < NEAR:
            return passing.at[step, origin, pl.ds(start, count)]
        return gathered.at[origin, pl.ds(far_row(step) + start, count)]

    def part_of(slot):
        return {6: (0, ROW // 2), 7: (ROW // 2, ROW // 2)}.get(slot, (0, ROW))

    def ring(slot, step):
        sign = 1 if slot % 2 == 0 else -1
        kind = slot // 2
        start, count = part_of(slot)
        hop = sign if kind == 0 else 2 * sign
        origin = level_of(high - {0: 0, 1: 0, 2: 1, 3: 2}[kind] * sign)
        if kind >= 2:
            source = held(step, origin, start, count)
        elif step < NEAR:
            source = tiles.at[lax.rem(parity + 1 + kind, 2), pl.ds(row_at(step), ROW)]
        elif kind == 0:
            source = other.at[pl.ds(far_row(step), ROW)]
        else:
            source = gathered.at[high, pl.ds(far_row(step), ROW)]
        return push(
            source, held(step, origin, start, count),
            ring_send.at[slot, step], ring_recv.at[slot, step], ring_at(hop),
        )

    def arrival(slot, step):
        sign = 1 if slot % 2 == 0 else -1
        reach = {0: 1, 1: 2, 2: 3, 3: 4}[slot // 2]
        target = held(step, level_of(high - reach * sign), *part_of(slot))
        push(target, target, ring_send.at[slot, step], ring_recv.at[slot, step], ring_at(1)).wait_recv()

    def send(slot, step):
        ring(slot, step).start()

    def hand_on(step):
        for slot in range(4):
            arrival(slot, step)
            send(slot + 4, step)

    for step in range(NEAR):
        for slot in range(4):
            send(slot, step)

    far_count = (ROWS - NEAR) * ROW
    for kind in range(2):

        def swap_step(step, _, kind=kind):
            to = lax.rem((line + NEAR) * ROW + step, SOURCES)
            source = tiles.at[lax.rem(parity + 1 + kind, 2), to]
            target = gathered.at[high, place] if kind else other.at[place]
            arrives = swap_recv.at[kind, ROWS - 1 - lax.div(step, ROW)]
            push(source, target, swap_send.at[kind], arrives, plane_at(to)).start()
            return 0

        lax.fori_loop(0, far_count, swap_step, 0)

    def landed(kind, step):
        some = pl.ds(far_row(step), ROW)
        whole = gathered.at[high, some] if kind else other.at[some]
        pltpu.make_async_copy(whole, whole, swap_recv.at[kind, step]).wait()

    def spread(step):
        for slot in range(4, 8):
            arrival(slot, step)
        own = tiles.at[parity, pl.ds(row_at(step), ROW)]
        own = pltpu.make_async_copy(own, passing.at[step, high], spread_recv.at[step])
        own.start()
        own.wait()

        def row_step(index, _):
            index = lax.rem(place + index, ROW)
            push(
                passing.at[step, :, index], gathered.at[:, place],
                swap_send.at[2 + step], swap_recv.at[step, 0], plane_at(row_at(step) + index),
            ).start()
            return 0

        lax.fori_loop(0 if step else 1, ROW, row_step, 0)
        if step == 0:
            pltpu.make_async_copy(
                passing.at[0, :, lax.rem(place, ROW)], gathered.at[:, place], swap_recv.at[0, 0]
            ).start()

    def far(*steps):
        for kind in range(2):
            for step in steps:
                landed(kind, step)
                send(2 * kind, step)
                send(2 * kind + 1, step)

    hand_on(0)
    hand_on(1)
    far(2, 3)
    spread(0)
    spread(1)
    hand_on(2)
    hand_on(3)
    for step in range(NEAR):
        some = gathered.at[:, pl.ds(row_at(-step), ROW)]
        pltpu.make_async_copy(some, some, swap_recv.at[step, 0]).wait()

    permute_copy.wait()
    turns_copy.wait()

    def turn(order, shard):
        shard = lax.rem(shard + 4, 4)
        turned = None
        for side in range(4):
            low, device = divmod(side, 2)
            held = gathered[2 * shard + low].reshape(COLUMNS, 2, TILE, LANES)[:, device]
            term = jnp.dot(
                held.reshape(COLUMNS * TILE, LANES), permute[side * LANES : (side + 1) * LANES],
                preferred_element_type=F32,
            )
            turned = term if turned is None else turned + term
        turned = turned.astype(BF16)
        for spectrum in range(4):
            for where in range(COLUMNS):
                row = (order * 4 + spectrum) * TILE
                out_ref[row : row + TILE, where * LANES : (where + 1) * LANES] = turned[
                    where * TILE : (where + 1) * TILE, spectrum * LANES : (spectrum + 1) * LANES
                ]

    def prepare(pair):
        rows = left_ref.shape[1]
        own = out_ref[pair * LANES : (pair + 1) * LANES, pl.ds(pl.multiple_of(feed * rows, rows), rows)]
        moved = jnp.dot(own.T, turns[...], preferred_element_type=F32).astype(BF16)
        for index in range(4):
            left_ref[index, :, pair * LANES : (pair + 1) * LANES] = moved[
                :, index * LANES : (index + 1) * LANES
            ]

    turn(0, feed)
    turn(1, feed - 1 + 2 * parity)
    prepare(0)
    for step in range(NEAR, ROWS):
        arrival(4, step)
        arrival(5, step)
    turn(2, feed + 1 - 2 * parity)
    for step in range(NEAR, ROWS):
        arrival(6, step)
        arrival(7, step)
    turn(3, feed + 2)
    prepare(1)
    for kind in range(2):
        some = tiles.at[0, pl.ds(0, far_count)]
        pltpu.make_async_copy(some, some, swap_send.at[kind]).wait()
    for step in range(NEAR):
        some = passing.at[step, :, pl.ds(0, ROW if step else ROW - 1)]
        pltpu.make_async_copy(some, some, swap_send.at[2 + step]).wait()
    for slot in range(8):
        for step in range(ROWS):
            ring(slot, step).wait_send()

    @pl.when(feed < RING // 2 - 1)
    def _():
        halo_copy.wait_send()


def correlate_kernel(signal_ref, left_ref, out_hbm, whole, sem):
    columns = 512
    count = whole.shape[3] // columns
    copies = []
    for index in range(4 * count):
        which, part, block = index // (2 * count), index // count % 2, index % count
        some = pl.ds(block * columns, columns)
        summed = jnp.dot(left_ref[2 * which + part], signal_ref[:, some], preferred_element_type=F32)
        whole[which, part, :, some] = summed.astype(BF16)
        copy = pltpu.make_async_copy(
            whole.at[which, part, :, some], out_hbm.at[which, part, :, some], sem.at[index]
        )
        copy.start()
        copies.append(copy)
    for copy in copies:
        copy.wait()


def on_device(voltages, taper, gains):
    table, select, permute, turns = (jnp.asarray(value) for value in constants())
    laid = voltages.reshape(IN_DEV, 2, 8, POINTS // LANES, LANES).transpose(0, 1, 3, 2, 4)
    laid = laid.reshape(IN_DEV, SPECS * POINTS // LANES, LANES)
    operands = (laid, taper, gains, table, select, permute, turns)
    inputs = SOURCES * 2 * IN_DEV
    rows = inputs // 4
    depth = 4 * 4 * TILE
    whole = pl.BlockSpec(memory_space=pltpu.VMEM)
    signals, left = pl.pallas_call(
        gather_kernel,
        out_shape=(
            jax.ShapeDtypeStruct((depth, inputs), BF16),
            jax.ShapeDtypeStruct((4, rows, depth), BF16),
        ),
        in_specs=[pl.BlockSpec(memory_space=pl.ANY)] * len(operands),
        out_specs=(whole, whole),
        scratch_shapes=[
            pltpu.VMEM((IN_DEV, PITCH, LANES), jnp.int32),
            pltpu.VMEM(taper.shape, F32),
            pltpu.VMEM(gains.shape, jnp.int32),
            pltpu.VMEM(table.shape, BF16),
            pltpu.VMEM(select.shape, BF16),
            pltpu.VMEM(permute.shape, BF16),
            pltpu.VMEM(turns.shape, BF16),
            pltpu.VMEM((2, 2, SPECS * IN_DEV, HALF), BF16),
            pltpu.VMEM((2, 2, LANES, HALF), BF16),
            pltpu.VMEM((2, LANES, LANES), F32),
            pltpu.VMEM((2 * SOURCES * TILE, LANES), F32),
            pltpu.VMEM((2, LANES, LANES), BF16),
            pltpu.VMEM((2, LANES, LANES), BF16),
            pltpu.VMEM((2, SOURCES, TILE, LANES), BF16),
            pltpu.VMEM((SOURCES, TILE, LANES), BF16),
            pltpu.VMEM((NEAR, RING, ROW, TILE, LANES), BF16),
            pltpu.VMEM((RING, SOURCES, TILE, LANES), BF16),
            pltpu.SemaphoreType.DMA((2, 2)),
            pltpu.SemaphoreType.DMA((len(operands) - 1,)),
            pltpu.SemaphoreType.DMA((2,)),
            pltpu.SemaphoreType.DMA((2 + NEAR,)),
            pltpu.SemaphoreType.DMA((2, ROWS)),
            pltpu.SemaphoreType.DMA((NEAR,)),
            pltpu.SemaphoreType.DMA((8, ROWS)),
            pltpu.SemaphoreType.DMA((8, ROWS)),
        ],
        compiler_params=pltpu.CompilerParams(
            collective_id=0, has_side_effects=True, vmem_limit_bytes=48 * 1024 * 1024
        ),
    )(*(pltpu.with_memory_space_constraint(value, pltpu.HBM) for value in operands))
    return pl.pallas_call(
        correlate_kernel,
        out_shape=jax.ShapeDtypeStruct((2, 2, rows, inputs), BF16),
        in_specs=[whole, whole],
        out_specs=pl.BlockSpec(memory_space=pl.ANY),
        scratch_shapes=[pltpu.VMEM((2, 2, rows, inputs), BF16), pltpu.SemaphoreType.DMA((16,))],
        compiler_params=pltpu.CompilerParams(vmem_limit_bytes=32 * 1024 * 1024),
    )(signals, left)


def solution(mesh):
    placed = (P("chan", "feed", None), P(), P("chan", None))
    return jax.shard_map(
        on_device,
        mesh=mesh,
        in_specs=placed,
        out_specs=P("chan", None, "feed", None),
        check_vma=False,
    )
```

```python
import functools
import math

import jax
import jax.numpy as jnp
import numpy as np
from jax import lax
from jax.experimental import pallas as pl
from jax.experimental.pallas import tpu as pltpu
from jax.sharding import PartitionSpec as P

MESH = pl.DeviceIdType.MESH
F32, BF16 = jnp.float32, jnp.bfloat16

POINTS = 2048
HALF = POINTS // 2
CHANNELS = 128
IN_DEV = 32
SPECS = 16
TAPS = 4
COLUMNS = 16
RING = 8
SOURCES = 2 * COLUMNS
TILE = 16
LANES = 128
ROW = 8
ROWS = SOURCES // ROW
NEAR = 2
PITCH = SPECS * POINTS // LANES + 8


def tile_channel():
    parity, place = np.divmod(np.arange(2 * SOURCES), SOURCES)
    column, core = np.divmod(place, 2)
    return 2 * (column * 4 + parity * 2 + core)


def split_two(value):
    high = value.astype(jnp.bfloat16)
    low = (value - high.astype(np.float64)).astype(jnp.bfloat16)
    return high, low


def constants():
    first = tile_channel()
    position = np.arange(HALF)
    tables, selects = [], []
    for which in range(2):
        order = first + which + 1
        phase = (order[:, None] * position[None, :]) % POINTS
        angle = phase * (2.0 * math.pi / POINTS)
        both = np.concatenate([np.cos(angle), -np.sin(angle)]) / math.sqrt(POINTS)
        tables.append(np.concatenate(split_two(both)))
        pick = (first + which)[:, None] == np.arange(CHANNELS)[None, :]
        selects.append(np.concatenate([pick, pick]))
    lane = np.arange(4 * LANES)
    device, rest = np.divmod(lane, LANES)
    spectrum, within = np.divmod(rest, IN_DEV)
    target = spectrum * LANES + device * IN_DEV + within
    permute = np.zeros((4 * LANES, 4 * LANES))
    permute[lane, target] = 1.0
    line = np.arange(LANES)
    within = line % TILE
    turns = []
    for which in range(2):
        chosen = (within // 4) % 2 == which
        same = np.diag(np.where(chosen, 1.0 / 64.0, 0.0))
        cross = np.zeros((LANES, LANES))
        cross[line, line ^ 8] = np.where(within < 8, -1.0 / 64.0, 1.0 / 64.0)
        turns += [same, cross * chosen[None, :]]
    return (
        np.stack(tables).astype(jnp.bfloat16),
        np.stack(selects).astype(jnp.bfloat16),
        permute.astype(jnp.bfloat16),
        np.concatenate(turns, axis=1).astype(jnp.bfloat16),
    )


def transposed_dot(left, right):
    return lax.dot_general(left, right, (((1,), (1,)), ((), ())), preferred_element_type=F32)


def gather_kernel(
    volt_hbm, taper_hbm, gain_hbm, table_hbm, select_hbm, permute_hbm, turns_hbm, out_ref, left_ref,
    volts, taper_ref, gain_ref, table, select_ref, permute, turns, sums, halo_sums, factors, stage, halo_out, halo_in, tiles, other, passing, gathered,
    load_sem, const_sem, halo_sem, swap_send, swap_recv, spread_recv, ring_send, ring_recv,
):
    chan, feed = lax.axis_index("chan"), lax.axis_index("feed")
    core = lax.rem(chan, 2)
    parity = lax.rem(lax.div(chan, 2), 2)
    column = lax.div(chan, 4)
    high = 2 * feed + parity
    place = column * 2 + core
    line = lax.div(place, ROW)

    def level_of(level):
        return lax.rem(level + RING, RING)

    def ring_at(hop):
        level = level_of(high + hop)
        return {"chan": column * 4 + lax.rem(level, 2) * 2 + core, "feed": lax.div(level, 2)}

    def plane_at(where):
        return {"chan": lax.div(where, 2) * 4 + parity * 2 + lax.rem(where, 2)}

    def load(half, part):
        some = pl.ds(part * IN_DEV // 2, IN_DEV // 2)
        lines = pl.ds(half * POINTS // LANES * 8, POINTS // LANES * 8)
        return pltpu.make_async_copy(
            volt_hbm.at[some, lines], volts.at[some, lines], load_sem.at[half, part]
        )

    small = (
        (taper_hbm, taper_ref), (table_hbm, table), (gain_hbm, gain_ref), (select_hbm, select_ref),
        (permute_hbm, permute), (turns_hbm, turns),
    )
    copies = [pltpu.make_async_copy(*pair, const_sem.at[n]) for n, pair in enumerate(small)]
    taper_copy, table_copy, gain_copy, select_copy, permute_copy, turns_copy = copies
    for copy in (taper_copy, gain_copy, select_copy):
        copy.start()
    for half in (1, 0):
        for part in range(2):
            load(half, part).start()
        if half == 1:
            table_copy.start()
    permute_copy.start()
    turns_copy.start()

    barrier = pltpu.get_barrier_semaphore()

    def greet(step, _):
        pl.semaphore_signal(
            barrier, inc=1, device_id=plane_at(lax.rem(place + step, SOURCES)), device_id_type=MESH
        )
        return 0

    lax.fori_loop(1, SOURCES, greet, 0)
    for hop in (-2, -1, 1, 2):
        pl.semaphore_signal(barrier, inc=1, device_id=ring_at(hop), device_id_type=MESH)

    flat = volts.reshape(IN_DEV * PITCH, LANES)

    def block(part, spectrum, tile):
        half, line = divmod(spectrum, 8)
        start = part * 16 * PITCH + half * POINTS // LANES * 8 + tile * 8 + line
        return flat[pl.ds(start, 16, stride=PITCH), :].astype(F32)

    def keep(target, row, lanes, first, second):
        for which, value in enumerate((first - second, first + second)):
            upper = value.astype(BF16)
            lower = (value - upper.astype(F32)).astype(BF16)
            target[which, 0, row, lanes] = upper
            target[which, 1, row, lanes] = lower

    def tapers(lanes):
        return [taper_ref[tap : tap + 1, lanes] for tap in range(TAPS)]

    def lanes_of(step):
        start = pl.multiple_of(step * LANES, LANES)
        return pl.ds(start, LANES), pl.ds(start + HALF, LANES)

    def halo_step(step, _, part):
        here, beyond = lanes_of(step)
        pair = []
        for lanes, tile in ((here, step), (beyond, step + HALF // LANES)):
            taps = tapers(lanes)
            held = [block(part, SPECS - 3 + back, tile) for back in range(3)]
            pair.append(
                [sum(taps[tap] * held[row + tap] for tap in range(3 - row)) for row in range(3)]
            )
        for row in range(3):
            keep(halo_sums, pl.ds(row * IN_DEV + part * 16, 16), here, pair[0][row], pair[1][row])
        return 0

    def main_step(step, _, part):
        here, beyond = lanes_of(step)
        first_taps, second_taps = tapers(here), tapers(beyond)
        first, second = [], []
        for row in range(SPECS):
            first.append(block(part, row, step))
            second.append(block(part, row, step + HALF // LANES))
            reach = [tap for tap in range(TAPS) if row - 3 + tap >= 0]
            one = sum(first_taps[tap] * first[row - 3 + tap] for tap in reach)
            two = sum(second_taps[tap] * second[row - 3 + tap] for tap in reach)
            keep(sums, pl.ds(row * IN_DEV + part * 16, 16), here, one, two)
        return 0

    def transform(source, which, rows):
        wide = transposed_dot(table[which], source[which, 0, rows])
        narrow = transposed_dot(table[which, :LANES], source[which, 1, rows])
        return wide[:LANES] + wide[LANES:] + narrow

    halo_sums[:, :, 3 * IN_DEV :] = jnp.zeros((2, 2, IN_DEV, HALF), BF16)
    gain_copy.wait()
    select_copy.wait()
    gain_rows = jnp.concatenate([gain_ref[...].astype(F32).astype(BF16)] * 4, axis=0)

    for which in range(2):
        factors[which] = transposed_dot(select_ref[which], gain_rows) * (1.0 / 4096.0)
    taper_copy.wait()
    for part in range(2):
        load(1, part).wait()
        lax.fori_loop(0, HALF // LANES, functools.partial(halo_step, part=part), 0)
    table_copy.wait()
    for which in range(2):
        halo_out[which] = transform(halo_sums, which, pl.ds(0, LANES)).astype(BF16)

    pl.semaphore_wait(barrier, SOURCES - 1 + 4)
    halo_copy = pltpu.make_async_remote_copy(
        src_ref=halo_out, dst_ref=halo_in, send_sem=halo_sem.at[0], recv_sem=halo_sem.at[1],
        device_id=ring_at(2), device_id_type=MESH,
    )

    @pl.when(feed < RING // 2 - 1)
    def _():
        halo_copy.start()

    for part in range(2):
        load(0, part).wait()
        lax.fori_loop(0, HALF // LANES, functools.partial(main_step, part=part), 0)

    def settle(which, group, value):
        value = value * factors[which]
        for side in range(2):
            rows = pl.ds(side * 8 + which * 4 + group, 2 * SOURCES, stride=TILE)
            stage[rows, :] = value[side * 2 * SOURCES : (side + 1) * 2 * SOURCES]

    firsts = []
    for which in range(2):
        for part in (1, 0):
            spectra = transform(sums, which, pl.ds(part * 2 * LANES, 2 * LANES))
            for within in range(2):
                value = spectra[:, within * LANES : (within + 1) * LANES]
                if part + within == 0:
                    firsts.append(value)
                else:
                    settle(which, part * 2 + within, value)

    @pl.when(feed == 0)
    def _():
        halo_in[...] = jnp.zeros_like(halo_in)

    @pl.when(feed > 0)
    def _():
        halo_copy.wait_recv()

    for which in range(2):
        settle(which, 0, firsts[which] + halo_in[which].astype(F32))
    tiles[...] = stage[...].astype(BF16).reshape(2, SOURCES, TILE, LANES)

    def push(source, target, send_sem, recv_sem, device):
        return pltpu.make_async_remote_copy(
            src_ref=source, dst_ref=target, send_sem=send_sem, recv_sem=recv_sem,
            device_id=device, device_id_type=MESH,
        )

    def row_at(offset):
        return lax.rem(line + offset + ROWS, ROWS) * ROW

    def far_row(step):
        return row_at(step - NEAR + 1)

    def held(step, origin):
        if step < NEAR:
            return passing.at[step, origin]
        return gathered.at[origin, pl.ds(far_row(step), ROW)]

    def used(slot, step):
        return slot < 6 or slot - 6 == step % 2

    def ring(slot, step):
        sign = 1 if slot % 2 == 0 else -1
        kind = slot // 2
        hop = sign if kind == 0 else 2 * sign
        origin = level_of(high - {0: 0, 1: 0, 2: 1, 3: 2}[kind] * sign)
        if kind >= 2:
            source = held(step, origin)
        elif step < NEAR:
            source = tiles.at[lax.rem(parity + 1 + kind, 2), pl.ds(row_at(step), ROW)]
        elif kind == 0:
            source = other.at[pl.ds(far_row(step), ROW)]
        else:
            source = gathered.at[high, pl.ds(far_row(step), ROW)]
        return push(
            source, held(step, origin),
            ring_send.at[slot, step], ring_recv.at[slot, step], ring_at(hop),
        )

    def arrival(slot, step):
        sign = 1 if slot % 2 == 0 else -1
        reach = {0: 1, 1: 2, 2: 3, 3: 4}[slot // 2]
        target = held(step, level_of(high - reach * sign))
        push(target, target, ring_send.at[slot, step], ring_recv.at[slot, step], ring_at(1)).wait_recv()

    def send(slot, step):
        ring(slot, step).start()

    def hand_on(step):
        for slot in range(4):
            arrival(slot, step)
            if used(slot + 4, step):
                send(slot + 4, step)

    for step in range(NEAR):
        for slot in range(4):
            send(slot, step)

    far_count = (ROWS - NEAR) * ROW
    for kind in range(2):

        def swap_step(step, _, kind=kind):
            to = lax.rem((line + NEAR) * ROW + step, SOURCES)
            source = tiles.at[lax.rem(parity + 1 + kind, 2), to]
            target = gathered.at[high, place] if kind else other.at[place]
            arrives = swap_recv.at[kind, ROWS - 1 - lax.div(step, ROW)]
            push(source, target, swap_send.at[kind], arrives, plane_at(to)).start()
            return 0

        lax.fori_loop(0, far_count, swap_step, 0)

    def landed(kind, step):
        some = pl.ds(far_row(step), ROW)
        whole = gathered.at[high, some] if kind else other.at[some]
        pltpu.make_async_copy(whole, whole, swap_recv.at[kind, step]).wait()

    def spread(step):
        for slot in range(4, 8):
            if used(slot, step):
                arrival(slot, step)
        own = tiles.at[parity, pl.ds(row_at(step), ROW)]
        own = pltpu.make_async_copy(own, passing.at[step, high], spread_recv.at[step])
        own.start()
        own.wait()

        def row_step(index, _):
            index = lax.rem(place + index, ROW)
            push(
                passing.at[step, :, index], gathered.at[:, place],
                swap_send.at[2 + step], swap_recv.at[step, 0], plane_at(row_at(step) + index),
            ).start()
            return 0

        lax.fori_loop(0 if step else 1, ROW, row_step, 0)
        if step == 0:
            pltpu.make_async_copy(
                passing.at[0, :, lax.rem(place, ROW)], gathered.at[:, place], swap_recv.at[0, 0]
            ).start()

    def far(*steps):
        for kind in range(2):
            for step in steps:
                landed(kind, step)
                send(2 * kind, step)
                send(2 * kind + 1, step)

    hand_on(0)
    hand_on(1)
    far(2, 3)
    spread(0)
    spread(1)
    hand_on(2)
    hand_on(3)
    for step in range(NEAR):
        some = gathered.at[:, pl.ds(row_at(-step), ROW)]
        pltpu.make_async_copy(some, some, swap_recv.at[step, 0]).wait()

    permute_copy.wait()
    turns_copy.wait()

    def turn(order, shard):
        shard = lax.rem(shard + 4, 4)
        turned = None
        for side in range(4):
            low, device = divmod(side, 2)
            held = gathered[2 * shard + low].reshape(COLUMNS, 2, TILE, LANES)[:, device]
            term = jnp.dot(
                held.reshape(COLUMNS * TILE, LANES), permute[side * LANES : (side + 1) * LANES],
                preferred_element_type=F32,
            )
            turned = term if turned is None else turned + term
        turned = turned.astype(BF16)
        for spectrum in range(4):
            for where in range(COLUMNS):
                row = (order * 4 + spectrum) * TILE
                out_ref[row : row + TILE, where * LANES : (where + 1) * LANES] = turned[
                    where * TILE : (where + 1) * TILE, spectrum * LANES : (spectrum + 1) * LANES
                ]

    def prepare(pair):
        rows = left_ref.shape[1]
        own = out_ref[pair * LANES : (pair + 1) * LANES, pl.ds(pl.multiple_of(feed * rows, rows), rows)]
        moved = jnp.dot(own.T, turns[...], preferred_element_type=F32).astype(BF16)
        for index in range(4):
            left_ref[index, :, pair * LANES : (pair + 1) * LANES] = moved[
                :, index * LANES : (index + 1) * LANES
            ]

    turn(0, feed)
    turn(1, feed - 1 + 2 * parity)
    prepare(0)
    for step in range(NEAR, ROWS):
        arrival(4, step)
        arrival(5, step)
    turn(2, feed + 1 - 2 * parity)
    for step in range(NEAR, ROWS):
        arrival(6 + step % 2, step)
    turn(3, feed + 2)
    prepare(1)
    for kind in range(2):
        some = tiles.at[0, pl.ds(0, far_count)]
        pltpu.make_async_copy(some, some, swap_send.at[kind]).wait()
    for step in range(NEAR):
        some = passing.at[step, :, pl.ds(0, ROW if step else ROW - 1)]
        pltpu.make_async_copy(some, some, swap_send.at[2 + step]).wait()
    for slot in range(8):
        for step in range(ROWS):
            if used(slot, step):
                ring(slot, step).wait_send()

    @pl.when(feed < RING // 2 - 1)
    def _():
        halo_copy.wait_send()


def correlate_kernel(signal_ref, left_ref, out_hbm, whole, sem):
    columns = 512
    count = whole.shape[3] // columns
    copies = []
    for index in range(4 * count):
        which, part, block = index // (2 * count), index // count % 2, index % count
        some = pl.ds(block * columns, columns)
        summed = jnp.dot(left_ref[2 * which + part], signal_ref[:, some], preferred_element_type=F32)
        whole[which, part, :, some] = summed.astype(BF16)
        copy = pltpu.make_async_copy(
            whole.at[which, part, :, some], out_hbm.at[which, part, :, some], sem.at[index]
        )
        copy.start()
        copies.append(copy)
    for copy in copies:
        copy.wait()


def on_device(voltages, taper, gains):
    table, select, permute, turns = (jnp.asarray(value) for value in constants())
    laid = voltages.reshape(IN_DEV, 2, 8, POINTS // LANES, LANES).transpose(0, 1, 3, 2, 4)
    laid = laid.reshape(IN_DEV, SPECS * POINTS // LANES, LANES)
    operands = (laid, taper, gains, table, select, permute, turns)
    inputs = SOURCES * 2 * IN_DEV
    rows = inputs // 4
    depth = 4 * 4 * TILE
    whole = pl.BlockSpec(memory_space=pltpu.VMEM)
    signals, left = pl.pallas_call(
        gather_kernel,
        out_shape=(
            jax.ShapeDtypeStruct((depth, inputs), BF16),
            jax.ShapeDtypeStruct((4, rows, depth), BF16),
        ),
        in_specs=[pl.BlockSpec(memory_space=pl.ANY)] * len(operands),
        out_specs=(whole, whole),
        scratch_shapes=[
            pltpu.VMEM((IN_DEV, PITCH, LANES), jnp.int32),
            pltpu.VMEM(taper.shape, F32),
            pltpu.VMEM(gains.shape, jnp.int32),
            pltpu.VMEM(table.shape, BF16),
            pltpu.VMEM(select.shape, BF16),
            pltpu.VMEM(permute.shape, BF16),
            pltpu.VMEM(turns.shape, BF16),
            pltpu.VMEM((2, 2, SPECS * IN_DEV, HALF), BF16),
            pltpu.VMEM((2, 2, LANES, HALF), BF16),
            pltpu.VMEM((2, LANES, LANES), F32),
            pltpu.VMEM((2 * SOURCES * TILE, LANES), F32),
            pltpu.VMEM((2, LANES, LANES), BF16),
            pltpu.VMEM((2, LANES, LANES), BF16),
            pltpu.VMEM((2, SOURCES, TILE, LANES), BF16),
            pltpu.VMEM((SOURCES, TILE, LANES), BF16),
            pltpu.VMEM((NEAR, RING, ROW, TILE, LANES), BF16),
            pltpu.VMEM((RING, SOURCES, TILE, LANES), BF16),
            pltpu.SemaphoreType.DMA((2, 2)),
            pltpu.SemaphoreType.DMA((len(operands) - 1,)),
            pltpu.SemaphoreType.DMA((2,)),
            pltpu.SemaphoreType.DMA((2 + NEAR,)),
            pltpu.SemaphoreType.DMA((2, ROWS)),
            pltpu.SemaphoreType.DMA((NEAR,)),
            pltpu.SemaphoreType.DMA((8, ROWS)),
            pltpu.SemaphoreType.DMA((8, ROWS)),
        ],
        compiler_params=pltpu.CompilerParams(
            collective_id=0, has_side_effects=True, vmem_limit_bytes=48 * 1024 * 1024
        ),
    )(*(pltpu.with_memory_space_constraint(value, pltpu.HBM) for value in operands))
    return pl.pallas_call(
        correlate_kernel,
        out_shape=jax.ShapeDtypeStruct((2, 2, rows, inputs), BF16),
        in_specs=[whole, whole],
        out_specs=pl.BlockSpec(memory_space=pl.ANY),
        scratch_shapes=[pltpu.VMEM((2, 2, rows, inputs), BF16), pltpu.SemaphoreType.DMA((16,))],
        compiler_params=pltpu.CompilerParams(vmem_limit_bytes=32 * 1024 * 1024),
    )(signals, left)


def solution(mesh):
    placed = (P("chan", "feed", None), P(), P("chan", None))
    return jax.shard_map(
        on_device,
        mesh=mesh,
        in_specs=placed,
        out_specs=P("chan", None, "feed", None),
        check_vma=False,
    )
```

```python
import functools
import math

import jax
import jax.numpy as jnp
import numpy as np
from jax import lax
from jax.experimental import pallas as pl
from jax.experimental.pallas import tpu as pltpu
from jax.sharding import PartitionSpec as P

MESH = pl.DeviceIdType.MESH
F32, BF16 = jnp.float32, jnp.bfloat16

POINTS = 2048
HALF = POINTS // 2
CHANNELS = 128
IN_DEV = 32
SPECS = 16
TAPS = 4
COLUMNS = 16
RING = 8
SOURCES = 2 * COLUMNS
TILE = 16
LANES = 128
ROW = 8
ROWS = SOURCES // ROW
NEAR = 2
PITCH = SPECS * POINTS // LANES + 8


def tile_channel():
    parity, place = np.divmod(np.arange(2 * SOURCES), SOURCES)
    column, core = np.divmod(place, 2)
    return 2 * (column * 4 + parity * 2 + core)


def split_two(value):
    high = value.astype(jnp.bfloat16)
    low = (value - high.astype(np.float64)).astype(jnp.bfloat16)
    return high, low


def constants():
    first = tile_channel()
    position = np.arange(HALF)
    tables, selects = [], []
    for which in range(2):
        order = first + which + 1
        phase = (order[:, None] * position[None, :]) % POINTS
        angle = phase * (2.0 * math.pi / POINTS)
        both = np.concatenate([np.cos(angle), -np.sin(angle)]) / math.sqrt(POINTS)
        tables.append(np.concatenate(split_two(both)))
        pick = (first + which)[:, None] == np.arange(CHANNELS)[None, :]
        selects.append(np.concatenate([pick, pick]))
    lane = np.arange(4 * LANES)
    device, rest = np.divmod(lane, LANES)
    spectrum, within = np.divmod(rest, IN_DEV)
    target = spectrum * LANES + device * IN_DEV + within
    permute = np.zeros((4 * LANES, 4 * LANES))
    permute[lane, target] = 1.0
    line = np.arange(LANES)
    within = line % TILE
    turns = []
    for which in range(2):
        chosen = (within // 4) % 2 == which
        same = np.diag(np.where(chosen, 1.0 / 64.0, 0.0))
        cross = np.zeros((LANES, LANES))
        cross[line, line ^ 8] = np.where(within < 8, -1.0 / 64.0, 1.0 / 64.0)
        turns += [same, cross * chosen[None, :]]
    return (
        np.stack(tables).astype(jnp.bfloat16),
        np.stack(selects).astype(jnp.bfloat16),
        permute.astype(jnp.bfloat16),
        np.concatenate(turns, axis=1).astype(jnp.bfloat16),
    )


def transposed_dot(left, right):
    return lax.dot_general(left, right, (((1,), (1,)), ((), ())), preferred_element_type=F32)


def gather_kernel(
    volt_hbm, taper_hbm, gain_hbm, table_hbm, select_hbm, permute_hbm, turns_hbm, out_ref, left_ref,
    volts, taper_ref, gain_ref, table, select_ref, permute, turns, sums, halo_sums, factors, stage, halo_out, halo_in, tiles, other, passing, gathered,
    load_sem, const_sem, halo_sem, swap_send, swap_recv, spread_recv, ring_send, ring_recv,
):
    chan, feed = lax.axis_index("chan"), lax.axis_index("feed")
    core = lax.rem(chan, 2)
    parity = lax.rem(lax.div(chan, 2), 2)
    column = lax.div(chan, 4)
    high = 2 * feed + parity
    place = column * 2 + core
    line = lax.div(place, ROW)

    def level_of(level):
        return lax.rem(level + RING, RING)

    def ring_at(hop):
        level = level_of(high + hop)
        return {"chan": column * 4 + lax.rem(level, 2) * 2 + core, "feed": lax.div(level, 2)}

    def plane_at(where):
        return {"chan": lax.div(where, 2) * 4 + parity * 2 + lax.rem(where, 2)}

    def load(half, part):
        some = pl.ds(part * IN_DEV // 2, IN_DEV // 2)
        lines = pl.ds(half * POINTS // LANES * 8, POINTS // LANES * 8)
        return pltpu.make_async_copy(
            volt_hbm.at[some, lines], volts.at[some, lines], load_sem.at[half, part]
        )

    small = (
        (taper_hbm, taper_ref), (table_hbm, table), (gain_hbm, gain_ref), (select_hbm, select_ref),
        (permute_hbm, permute), (turns_hbm, turns),
    )
    copies = [pltpu.make_async_copy(*pair, const_sem.at[n]) for n, pair in enumerate(small)]
    taper_copy, table_copy, gain_copy, select_copy, permute_copy, turns_copy = copies
    for copy in (taper_copy, gain_copy, select_copy):
        copy.start()
    for half in (1, 0):
        for part in range(2):
            load(half, part).start(priority=part)
        if half == 1:
            table_copy.start()
    permute_copy.start()
    turns_copy.start()

    barrier = pltpu.get_barrier_semaphore()

    def greet(step, _):
        pl.semaphore_signal(
            barrier, inc=1, device_id=plane_at(lax.rem(place + step, SOURCES)), device_id_type=MESH
        )
        return 0

    lax.fori_loop(1, SOURCES, greet, 0)
    for hop in (-2, -1, 1, 2):
        pl.semaphore_signal(barrier, inc=1, device_id=ring_at(hop), device_id_type=MESH)

    flat = volts.reshape(IN_DEV * PITCH, LANES)

    def block(part, spectrum, tile):
        half, line = divmod(spectrum, 8)
        start = part * 16 * PITCH + half * POINTS // LANES * 8 + tile * 8 + line
        return flat[pl.ds(start, 16, stride=PITCH), :].astype(F32)

    def keep(target, row, lanes, first, second):
        for which, value in enumerate((first - second, first + second)):
            upper = value.astype(BF16)
            lower = (value - upper.astype(F32)).astype(BF16)
            target[which, 0, row, lanes] = upper
            target[which, 1, row, lanes] = lower

    def tapers(lanes):
        return [taper_ref[tap : tap + 1, lanes] for tap in range(TAPS)]

    def lanes_of(step):
        start = pl.multiple_of(step * LANES, LANES)
        return pl.ds(start, LANES), pl.ds(start + HALF, LANES)

    def halo_step(step, _, part):
        here, beyond = lanes_of(step)
        pair = []
        for lanes, tile in ((here, step), (beyond, step + HALF // LANES)):
            taps = tapers(lanes)
            held = [block(part, SPECS - 3 + back, tile) for back in range(3)]
            pair.append(
                [sum(taps[tap] * held[row + tap] for tap in range(3 - row)) for row in range(3)]
            )
        for row in range(3):
            keep(halo_sums, pl.ds(row * IN_DEV + part * 16, 16), here, pair[0][row], pair[1][row])
        return 0

    def main_step(step, _, part):
        here, beyond = lanes_of(step)
        first_taps, second_taps = tapers(here), tapers(beyond)
        first, second = [], []
        for row in range(SPECS):
            first.append(block(part, row, step))
            second.append(block(part, row, step + HALF // LANES))
            reach = [tap for tap in range(TAPS) if row - 3 + tap >= 0]
            one = sum(first_taps[tap] * first[row - 3 + tap] for tap in reach)
            two = sum(second_taps[tap] * second[row - 3 + tap] for tap in reach)
            keep(sums, pl.ds(row * IN_DEV + part * 16, 16), here, one, two)
        return 0

    def transform(source, which, rows):
        wide = transposed_dot(table[which], source[which, 0, rows])
        narrow = transposed_dot(table[which, :LANES], source[which, 1, rows])
        return wide[:LANES] + wide[LANES:] + narrow

    halo_sums[:, :, 3 * IN_DEV :] = jnp.zeros((2, 2, IN_DEV, HALF), BF16)
    gain_copy.wait()
    select_copy.wait()
    gain_rows = jnp.concatenate([gain_ref[...].astype(F32).astype(BF16)] * 4, axis=0)

    for which in range(2):
        factors[which] = transposed_dot(select_ref[which], gain_rows) * (1.0 / 4096.0)
    taper_copy.wait()
    for part in range(2):
        load(1, part).wait()
        lax.fori_loop(0, HALF // LANES, functools.partial(halo_step, part=part), 0)
    table_copy.wait()
    for which in range(2):
        halo_out[which] = transform(halo_sums, which, pl.ds(0, LANES)).astype(BF16)

    pl.semaphore_wait(barrier, SOURCES - 1 + 4)
    halo_copy = pltpu.make_async_remote_copy(
        src_ref=halo_out, dst_ref=halo_in, send_sem=halo_sem.at[0], recv_sem=halo_sem.at[1],
        device_id=ring_at(2), device_id_type=MESH,
    )

    @pl.when(feed < RING // 2 - 1)
    def _():
        halo_copy.start()

    for part in range(2):
        load(0, part).wait()
        lax.fori_loop(0, HALF // LANES, functools.partial(main_step, part=part), 0)

    def settle(which, group, value):
        value = value * factors[which]
        for side in range(2):
            rows = pl.ds(side * 8 + which * 4 + group, 2 * SOURCES, stride=TILE)
            stage[rows, :] = value[side * 2 * SOURCES : (side + 1) * 2 * SOURCES]

    firsts = []
    for which in range(2):
        for part in (1, 0):
            spectra = transform(sums, which, pl.ds(part * 2 * LANES, 2 * LANES))
            for within in range(2):
                value = spectra[:, within * LANES : (within + 1) * LANES]
                if part + within == 0:
                    firsts.append(value)
                else:
                    settle(which, part * 2 + within, value)

    @pl.when(feed == 0)
    def _():
        halo_in[...] = jnp.zeros_like(halo_in)

    @pl.when(feed > 0)
    def _():
        halo_copy.wait_recv()

    for which in range(2):
        settle(which, 0, firsts[which] + halo_in[which].astype(F32))
    tiles[...] = stage[...].astype(BF16).reshape(2, SOURCES, TILE, LANES)

    def push(source, target, send_sem, recv_sem, device):
        return pltpu.make_async_remote_copy(
            src_ref=source, dst_ref=target, send_sem=send_sem, recv_sem=recv_sem,
            device_id=device, device_id_type=MESH,
        )

    def row_at(offset):
        return lax.rem(line + offset + ROWS, ROWS) * ROW

    def far_row(step):
        return row_at(step - NEAR + 1)

    def held(step, origin, start=0, count=ROW):
        if step < NEAR:
            return passing.at[step, origin, pl.ds(start, count)]
        return gathered.at[origin, pl.ds(far_row(step) + start, count)]

    def part_of(slot):
        return {6: (0, ROW // 2), 7: (ROW // 2, ROW // 2)}.get(slot, (0, ROW))

    def ring(slot, step):
        sign = 1 if slot % 2 == 0 else -1
        kind = slot // 2
        start, count = part_of(slot)
        hop = sign if kind == 0 else 2 * sign
        origin = level_of(high - {0: 0, 1: 0, 2: 1, 3: 2}[kind] * sign)
        if kind >= 2:
            source = held(step, origin, start, count)
        elif step < NEAR:
            source = tiles.at[lax.rem(parity + 1 + kind, 2), pl.ds(row_at(step), ROW)]
        elif kind == 0:
            source = other.at[pl.ds(far_row(step), ROW)]
        else:
            source = gathered.at[high, pl.ds(far_row(step), ROW)]
        return push(
            source, held(step, origin, start, count),
            ring_send.at[slot, step], ring_recv.at[slot, step], ring_at(hop),
        )

    def arrival(slot, step):
        sign = 1 if slot % 2 == 0 else -1
        reach = {0: 1, 1: 2, 2: 3, 3: 4}[slot // 2]
        target = held(step, level_of(high - reach * sign), *part_of(slot))
        push(target, target, ring_send.at[slot, step], ring_recv.at[slot, step], ring_at(1)).wait_recv()

    def send(slot, step):
        ring(slot, step).start()

    def hand_on(step):
        for slot in range(4):
            arrival(slot, step)
            send(slot + 4, step)

    for step in range(NEAR):
        for slot in range(4):
            send(slot, step)

    far_count = (ROWS - NEAR) * ROW
    for kind in range(2):

        def swap_step(step, _, kind=kind):
            to = lax.rem((line + NEAR) * ROW + step, SOURCES)
            source = tiles.at[lax.rem(parity + 1 + kind, 2), to]
            target = gathered.at[high, place] if kind else other.at[place]
            arrives = swap_recv.at[kind, ROWS - 1 - lax.div(step, ROW)]
            push(source, target, swap_send.at[kind], arrives, plane_at(to)).start()
            return 0

        lax.fori_loop(0, far_count, swap_step, 0)

    def landed(kind, step):
        some = pl.ds(far_row(step), ROW)
        whole = gathered.at[high, some] if kind else other.at[some]
        pltpu.make_async_copy(whole, whole, swap_recv.at[kind, step]).wait()

    def spread(step):
        for slot in range(4, 8):
            arrival(slot, step)
        own = tiles.at[parity, pl.ds(row_at(step), ROW)]
        own = pltpu.make_async_copy(own, passing.at[step, high], spread_recv.at[step])
        own.start()
        own.wait()

        def row_step(index, _):
            index = lax.rem(place + index, ROW)
            push(
                passing.at[step, :, index], gathered.at[:, place],
                swap_send.at[2 + step], swap_recv.at[step, 0], plane_at(row_at(step) + index),
            ).start()
            return 0

        lax.fori_loop(0 if step else 1, ROW, row_step, 0)
        if step == 0:
            pltpu.make_async_copy(
                passing.at[0, :, lax.rem(place, ROW)], gathered.at[:, place], swap_recv.at[0, 0]
            ).start()

    def far(*steps):
        for kind in range(2):
            for step in steps:
                landed(kind, step)
                send(2 * kind, step)
                send(2 * kind + 1, step)

    hand_on(0)
    hand_on(1)
    far(2, 3)
    spread(0)
    spread(1)
    hand_on(2)
    hand_on(3)
    for step in range(NEAR):
        some = gathered.at[:, pl.ds(row_at(-step), ROW)]
        pltpu.make_async_copy(some, some, swap_recv.at[step, 0]).wait()

    permute_copy.wait()
    turns_copy.wait()

    def turn(order, shard):
        shard = lax.rem(shard + 4, 4)
        turned = None
        for side in range(4):
            low, device = divmod(side, 2)
            held = gathered[2 * shard + low].reshape(COLUMNS, 2, TILE, LANES)[:, device]
            term = jnp.dot(
                held.reshape(COLUMNS * TILE, LANES), permute[side * LANES : (side + 1) * LANES],
                preferred_element_type=F32,
            )
            turned = term if turned is None else turned + term
        turned = turned.astype(BF16)
        for spectrum in range(4):
            for where in range(COLUMNS):
                row = (order * 4 + spectrum) * TILE
                out_ref[row : row + TILE, where * LANES : (where + 1) * LANES] = turned[
                    where * TILE : (where + 1) * TILE, spectrum * LANES : (spectrum + 1) * LANES
                ]

    def prepare(pair):
        rows = left_ref.shape[1]
        own = out_ref[pair * LANES : (pair + 1) * LANES, pl.ds(pl.multiple_of(feed * rows, rows), rows)]
        moved = jnp.dot(own.T, turns[...], preferred_element_type=F32).astype(BF16)
        for index in range(4):
            left_ref[index, :, pair * LANES : (pair + 1) * LANES] = moved[
                :, index * LANES : (index + 1) * LANES
            ]

    turn(0, feed)
    turn(1, feed - 1 + 2 * parity)
    prepare(0)
    for step in range(NEAR, ROWS):
        arrival(4, step)
        arrival(5, step)
    turn(2, feed + 1 - 2 * parity)
    for step in range(NEAR, ROWS):
        arrival(6, step)
        arrival(7, step)
    turn(3, feed + 2)
    prepare(1)
    for kind in range(2):
        some = tiles.at[0, pl.ds(0, far_count)]
        pltpu.make_async_copy(some, some, swap_send.at[kind]).wait()
    for step in range(NEAR):
        some = passing.at[step, :, pl.ds(0, ROW if step else ROW - 1)]
        pltpu.make_async_copy(some, some, swap_send.at[2 + step]).wait()
    for slot in range(8):
        for step in range(ROWS):
            ring(slot, step).wait_send()

    @pl.when(feed < RING // 2 - 1)
    def _():
        halo_copy.wait_send()


def correlate_kernel(signal_ref, left_ref, out_hbm, whole, sem):
    columns = 512
    count = whole.shape[3] // columns
    copies = []
    for index in range(4 * count):
        which, part, block = index // (2 * count), index // count % 2, index % count
        some = pl.ds(block * columns, columns)
        summed = jnp.dot(left_ref[2 * which + part], signal_ref[:, some], preferred_element_type=F32)
        whole[which, part, :, some] = summed.astype(BF16)
        copy = pltpu.make_async_copy(
            whole.at[which, part, :, some], out_hbm.at[which, part, :, some], sem.at[index]
        )
        copy.start()
        copies.append(copy)
    for copy in copies:
        copy.wait()


def on_device(voltages, taper, gains):
    table, select, permute, turns = (jnp.asarray(value) for value in constants())
    laid = voltages.reshape(IN_DEV, 2, 8, POINTS // LANES, LANES).transpose(0, 1, 3, 2, 4)
    laid = laid.reshape(IN_DEV, SPECS * POINTS // LANES, LANES)
    operands = (laid, taper, gains, table, select, permute, turns)
    inputs = SOURCES * 2 * IN_DEV
    rows = inputs // 4
    depth = 4 * 4 * TILE
    whole = pl.BlockSpec(memory_space=pltpu.VMEM)
    signals, left = pl.pallas_call(
        gather_kernel,
        out_shape=(
            jax.ShapeDtypeStruct((depth, inputs), BF16),
            jax.ShapeDtypeStruct((4, rows, depth), BF16),
        ),
        in_specs=[pl.BlockSpec(memory_space=pl.ANY)] * len(operands),
        out_specs=(whole, whole),
        scratch_shapes=[
            pltpu.VMEM((IN_DEV, PITCH, LANES), jnp.int32),
            pltpu.VMEM(taper.shape, F32),
            pltpu.VMEM(gains.shape, jnp.int32),
            pltpu.VMEM(table.shape, BF16),
            pltpu.VMEM(select.shape, BF16),
            pltpu.VMEM(permute.shape, BF16),
            pltpu.VMEM(turns.shape, BF16),
            pltpu.VMEM((2, 2, SPECS * IN_DEV, HALF), BF16),
            pltpu.VMEM((2, 2, LANES, HALF), BF16),
            pltpu.VMEM((2, LANES, LANES), F32),
            pltpu.VMEM((2 * SOURCES * TILE, LANES), F32),
            pltpu.VMEM((2, LANES, LANES), BF16),
            pltpu.VMEM((2, LANES, LANES), BF16),
            pltpu.VMEM((2, SOURCES, TILE, LANES), BF16),
            pltpu.VMEM((SOURCES, TILE, LANES), BF16),
            pltpu.VMEM((NEAR, RING, ROW, TILE, LANES), BF16),
            pltpu.VMEM((RING, SOURCES, TILE, LANES), BF16),
            pltpu.SemaphoreType.DMA((2, 2)),
            pltpu.SemaphoreType.DMA((len(operands) - 1,)),
            pltpu.SemaphoreType.DMA((2,)),
            pltpu.SemaphoreType.DMA((2 + NEAR,)),
            pltpu.SemaphoreType.DMA((2, ROWS)),
            pltpu.SemaphoreType.DMA((NEAR,)),
            pltpu.SemaphoreType.DMA((8, ROWS)),
            pltpu.SemaphoreType.DMA((8, ROWS)),
        ],
        compiler_params=pltpu.CompilerParams(
            collective_id=0, has_side_effects=True, vmem_limit_bytes=48 * 1024 * 1024
        ),
    )(*(pltpu.with_memory_space_constraint(value, pltpu.HBM) for value in operands))
    return pl.pallas_call(
        correlate_kernel,
        out_shape=jax.ShapeDtypeStruct((2, 2, rows, inputs), BF16),
        in_specs=[whole, whole],
        out_specs=pl.BlockSpec(memory_space=pl.ANY),
        scratch_shapes=[pltpu.VMEM((2, 2, rows, inputs), BF16), pltpu.SemaphoreType.DMA((16,))],
        compiler_params=pltpu.CompilerParams(vmem_limit_bytes=32 * 1024 * 1024),
    )(signals, left)


def solution(mesh):
    placed = (P("chan", "feed", None), P(), P("chan", None))
    return jax.shard_map(
        on_device,
        mesh=mesh,
        in_specs=placed,
        out_specs=P("chan", None, "feed", None),
        check_vma=False,
    )
```
